32 devices in a mesh: frame: 2 (over y), space: 8 (over z, x), dp: 2 (over core).
Axes of the slice: x: 2, y: 2, z: 4, core: 2. Of those that a mesh axis runs over, the one named last changes fastest.
Arguments:
- frames_in: bfloat16 [4, 1024, 768], P(('dp', 'frame'), 'space'), parts along dimension 0, may hold values from -6 to 6
- cotangent: bfloat16 [4, 1024, 768], P(('dp', 'frame'), 'space'), parts along dimension 0, may hold values from -6 to 6
- w_qkv_space: bfloat16 [768, 2304], P('space'), may hold values from -0.21875 to 0.21875
- w_out_space: bfloat16 [768, 768], P('space'), may hold values from -0.875 to 0.875
- w_qkv_time: bfloat16 [768, 2304], P('space'), may hold values from -0.21875 to 0.21875
- w_out_time: bfloat16 [768, 768], P('space'), may hold values from -0.21875 to 0.21875
- neighbours: int32 [8, 4], replicated, may hold values from 0 to 7, as said below
Outputs:
- frames_out: bfloat16 [4, 1024, 768], P(('dp', 'frame'), 'space'), parts along dimension 0
- grad_frames: bfloat16 [4, 1024, 768], P(('dp', 'frame'), 'space'), parts along dimension 0
The draws below stay inside these ranges and needn't reach their ends.
There are 2 independent parts, one for each index of `dp`. The reference program is written for one: setup_inputs(seed, part) draws one part's arguments, and reference() takes and returns one part's arrays. A program takes and returns all parts, laid end to end along the dimension named above; an argument that names none is the same for every part. Nothing has to cross between parts.
Inputs may be any that keep to these rules, and one draw needn't show every extreme that they name: `neighbours`: row b lists block b first; every entry c satisfies |c - b| <= 1; entries may repeat, and a repeated entry counts once.
All inputs are finite; a program needn't handle non-finite values.
Results may differ from the reference program's by a relative error of at most 0.023.
Values may be sent and summed in bfloat16 or wider, within the bound.
A program may use at most 64 MiB of HBM per device.

```python
import jax
import jax.numpy as jnp
from jax import lax

D = 768
HEADS = 12
HD = 64
BLOCK = 128
KNB = 4
BLK_DEV = 1
NBLK = 8
FTOK = 1024
FRAMES = 2
N_SPACE = 8


def draw_neighbours(key, part):
    block_ids = jnp.arange(NBLK, dtype=jnp.int32)
    offsets = jax.random.randint(key, (NBLK, KNB - 1), -BLK_DEV, BLK_DEV + 1, dtype=jnp.int32)
    others = jnp.clip(block_ids[:, None] + offsets, 0, NBLK - 1)
    return jnp.concatenate([block_ids[:, None], others], axis=1).astype(jnp.int32)


def block_levels(rng, dims, cuts, smallest, largest):
    def one(dim, shards_of):
        draws = jax.random.uniform(jax.random.fold_in(jax.random.fold_in(rng, 6), dim), (shards_of,), jnp.float32, smallest / len(cuts), largest / len(cuts))
        return jnp.repeat(jnp.exp(draws), dims[dim] // shards_of).reshape((-1,) + (1,) * (len(dims) - dim - 1))

    loudness = one(*cuts[0])
    for cut in cuts[1:]:
        loudness = loudness * one(*cut)
    return loudness


def normal_values(own_key, extent, deviation, reach, cuts=(), held_as=jnp.bfloat16):
    drawn = deviation * jax.random.normal(own_key, extent, jnp.float32)
    if cuts:
        drawn = drawn * block_levels(own_key, extent, cuts, -0.22, 0.18)
    return jnp.clip(drawn, -reach, reach).astype(held_as)


def setup_inputs(seed: int = 0, part: int = 0) -> dict:
    seeds = jax.random.split(jax.random.key(seed), 8)
    part_splits = jax.random.split(jax.random.fold_in(seeds[7], part), 8)
    frames_in = normal_values(part_splits[0], (FRAMES, FTOK, D), 1.0, 6.0, ((0, 2), (1, 8)))
    cotangent = normal_values(part_splits[1], (FRAMES, FTOK, D), 1.0, 6.0, ((0, 2), (1, 8)))
    w_qkv_space = normal_values(seeds[2], (D, 3 * D), D ** -0.5, 0.21875, ((0, 8),))
    w_out_space = normal_values(seeds[3], (D, D), (D // 16) ** -0.5, 0.875, ((0, 8),))
    w_qkv_time = normal_values(seeds[4], (D, 3 * D), D ** -0.5, 0.21875, ((0, 8),))
    w_out_time = normal_values(seeds[5], (D, D), D ** -0.5, 0.21875, ((0, 8),))
    neighbours = draw_neighbours(jax.random.fold_in(seeds[7], 71), part)
    return dict(frames_in=frames_in, cotangent=cotangent, w_qkv_space=w_qkv_space, w_out_space=w_out_space, w_qkv_time=w_qkv_time, w_out_time=w_out_time, neighbours=neighbours)


EPS = 1e-06

def widen(array):
    return lax.optimization_barrier(array).astype(jnp.float32)

def rms_norm(row_data):
    values = row_data.astype(jnp.float32)
    factor = lax.rsqrt(lax.optimization_barrier(jnp.mean(values * values, axis=-1, keepdims=True)) + EPS)
    return (values * factor).astype(jnp.bfloat16)

def rms_back(row_data, upstream):
    values = row_data.astype(jnp.float32)
    factor = lax.rsqrt(lax.optimization_barrier(jnp.mean(values * values, axis=-1, keepdims=True)) + EPS)
    inner_mean = lax.optimization_barrier(jnp.mean(values * upstream, axis=-1, keepdims=True))
    return factor * upstream - values * factor ** 3 * inner_mean

def block_mask(neighbour_rows, first_id):
    block_count = neighbour_rows.shape[0]
    candidate = first_id + jnp.arange(3 * block_count, dtype=jnp.int32)
    matches = jnp.any(neighbour_rows[:, :, None] == candidate[None, None, :], axis=1)
    return jnp.repeat(jnp.repeat(matches, BLOCK, axis=0), BLOCK, axis=1)

def space_attend(queries, key_rows, value_rows, allowed):
    score_scale = HD ** (-0.5)
    query_count = queries.shape[0]
    key_count = key_rows.shape[0]
    output_list = []
    total_list = []
    for head_pair in range(HEADS // 2):
        start_col = head_pair * 2 * HD
        stop_col = start_col + 2 * HD
        query_part = widen(queries[:, start_col:stop_col].reshape(query_count, 2, HD))
        key_part = widen(key_rows[:, start_col:stop_col].reshape(key_count, 2, HD))
        value_part = widen(value_rows[:, start_col:stop_col].reshape(key_count, 2, HD))
        scores = jnp.einsum('sgh,tgh->gst', query_part, key_part) * score_scale
        exponent = jnp.where(allowed[None], jnp.exp(scores), 0.0)
        totals = lax.optimization_barrier(jnp.sum(exponent, axis=-1))
        probability = (exponent / totals[:, :, None]).astype(jnp.bfloat16)
        combined = jnp.einsum('gst,tgh->sgh', widen(probability), value_part)
        output_list.append(combined.astype(jnp.bfloat16).reshape(query_count, 2 * HD))
        total_list.append(totals)
    return (jnp.concatenate(output_list, axis=1), jnp.concatenate(total_list, axis=0))

def space_back(queries, key_rows, value_rows, allowed, totals, attended, grad_attended):
    score_scale = HD ** (-0.5)
    query_count = queries.shape[0]
    key_count = key_rows.shape[0]
    query_list = []
    key_list = []
    value_list = []
    for head_pair in range(HEADS // 2):
        start_col = head_pair * 2 * HD
        stop_col = start_col + 2 * HD
        query_part = widen(queries[:, start_col:stop_col].reshape(query_count, 2, HD))
        key_part = widen(key_rows[:, start_col:stop_col].reshape(key_count, 2, HD))
        value_part = widen(value_rows[:, start_col:stop_col].reshape(key_count, 2, HD))
        out_part = widen(attended[:, start_col:stop_col].reshape(query_count, 2, HD))
        grad_part = widen(grad_attended[:, start_col:stop_col].reshape(query_count, 2, HD))
        scores = jnp.einsum('sgh,tgh->gst', query_part, key_part) * score_scale
        exponent = jnp.where(allowed[None], jnp.exp(scores), 0.0)
        weight = exponent / totals[2 * head_pair:2 * head_pair + 2, :, None]
        probability = weight.astype(jnp.bfloat16)
        prob_grad = jnp.einsum('sgh,tgh->gst', grad_part, value_part)
        row_delta = jnp.einsum('sgh,sgh->gs', grad_part, out_part)
        score_grad = (weight * (prob_grad - row_delta[:, :, None])).astype(jnp.bfloat16)
        query_grad = jnp.einsum('gst,tgh->sgh', widen(score_grad), key_part) * score_scale
        key_grad = jnp.einsum('gst,sgh->tgh', widen(score_grad), query_part) * score_scale
        value_grad = jnp.einsum('gst,sgh->tgh', widen(probability), grad_part)
        query_list.append(query_grad.astype(jnp.bfloat16).reshape(query_count, 2 * HD))
        key_list.append(key_grad.reshape(key_count, 2 * HD))
        value_list.append(value_grad.reshape(key_count, 2 * HD))
    return (jnp.concatenate(query_list, axis=1), jnp.concatenate(key_list, axis=1), jnp.concatenate(value_list, axis=1))

def time_attend(queries, key_rows, value_rows):
    frame_count, position_count, feature_count = queries.shape
    split_shape = (frame_count, position_count, HEADS, HD)
    score_scale = HD ** (-0.5)
    scores = jnp.einsum('fphd,gphd->phfg', widen(queries.reshape(split_shape)), widen(key_rows.reshape(split_shape))) * score_scale
    causal = jnp.arange(frame_count)[:, None] >= jnp.arange(frame_count)[None, :]
    exponent = jnp.where(causal, jnp.exp(scores), 0.0)
    totals = lax.optimization_barrier(jnp.sum(exponent, axis=-1))
    probability = (exponent / totals[..., None]).astype(jnp.bfloat16)
    combined = jnp.einsum('phfg,gphd->fphd', widen(probability), widen(value_rows.reshape(split_shape)))
    return (combined.astype(jnp.bfloat16).reshape(frame_count, position_count, feature_count), totals)

def time_back(queries, key_rows, value_rows, attended, grad_attended, totals):
    frame_count, position_count, feature_count = queries.shape
    split_shape = (frame_count, position_count, HEADS, HD)
    score_scale = HD ** (-0.5)
    query_four = widen(queries.reshape(split_shape))
    key_four = widen(key_rows.reshape(split_shape))
    value_four = widen(value_rows.reshape(split_shape))
    out_four = widen(attended.reshape(split_shape))
    grad_four = widen(grad_attended.reshape(split_shape))
    scores = jnp.einsum('fphd,gphd->phfg', query_four, key_four) * score_scale
    causal = jnp.arange(frame_count)[:, None] >= jnp.arange(frame_count)[None, :]
    exponent = jnp.where(causal, jnp.exp(scores), 0.0)
    weight = exponent / totals[..., None]
    probability = weight.astype(jnp.bfloat16)
    prob_grad = jnp.einsum('fphd,gphd->phfg', grad_four, value_four)
    row_delta = jnp.einsum('fphd,fphd->phf', grad_four, out_four)
    score_grad = (weight * (prob_grad - row_delta[..., None])).astype(jnp.bfloat16)
    query_grad = jnp.einsum('phfg,gphd->fphd', widen(score_grad), key_four) * score_scale
    key_grad = jnp.einsum('phfg,fphd->gphd', widen(score_grad), query_four) * score_scale
    value_grad = jnp.einsum('phfg,fphd->gphd', widen(probability), grad_four)
    pieces = [gradient.astype(jnp.bfloat16).reshape(frame_count, position_count, feature_count) for gradient in (query_grad, key_grad, value_grad)]
    return jnp.concatenate(pieces, axis=-1)

def time_block(stream_rows, grad_rows, qkv_weight, out_weight):
    frame_count, position_count, feature_count = stream_rows.shape
    flat_count = frame_count * position_count
    normed = rms_norm(stream_rows).reshape(flat_count, feature_count)
    projected = jnp.dot(normed, qkv_weight, preferred_element_type=jnp.float32).astype(jnp.bfloat16)
    projected = projected.reshape(frame_count, position_count, 3 * feature_count)
    queries = projected[..., :feature_count]
    key_rows = projected[..., feature_count:2 * feature_count]
    value_rows = projected[..., 2 * feature_count:]
    attended, totals = time_attend(queries, key_rows, value_rows)
    update = jnp.dot(attended.reshape(flat_count, feature_count), out_weight, preferred_element_type=jnp.float32)
    out_rows = (stream_rows.astype(jnp.float32) + update.reshape(stream_rows.shape)).astype(jnp.bfloat16)
    grad_attended = jnp.dot(grad_rows.reshape(flat_count, feature_count), out_weight.T, preferred_element_type=jnp.float32).astype(jnp.bfloat16).reshape(stream_rows.shape)
    gradients = time_back(queries, key_rows, value_rows, attended, grad_attended, totals)
    grad_normed = jnp.dot(gradients.reshape(flat_count, 3 * feature_count), qkv_weight.T, preferred_element_type=jnp.float32).reshape(stream_rows.shape)
    grad_stream = (grad_rows.astype(jnp.float32) + rms_back(stream_rows, grad_normed)).astype(jnp.bfloat16)
    return (out_rows, grad_stream)

def windows(shards):
    zero_shard = jnp.zeros((1,) + shards.shape[1:], shards.dtype)
    padded = jnp.concatenate([zero_shard, shards, zero_shard], axis=0)
    return jnp.concatenate([padded[:-2], padded[1:-1], padded[2:]], axis=1)

def combine(partial_value, shard):
    own_part = partial_value[:, shard:2 * shard]
    lower_part = lax.optimization_barrier(partial_value[:, :shard].astype(jnp.bfloat16))
    upper_part = lax.optimization_barrier(partial_value[:, 2 * shard:].astype(jnp.bfloat16))
    zero_shard = jnp.zeros((1,) + lower_part.shape[1:], jnp.bfloat16)
    from_prev = jnp.concatenate([zero_shard, upper_part[:-1]], axis=0)
    from_next = jnp.concatenate([lower_part[1:], zero_shard], axis=0)
    summed = own_part + from_prev.astype(jnp.float32) + from_next.astype(jnp.float32)
    return summed.astype(jnp.bfloat16)

def reference(frames_in, cotangent, w_qkv_space, w_out_space, w_qkv_time, w_out_time, neighbours):
    frame_count, frame_tokens, feature_count = frames_in.shape
    shard = BLK_DEV * BLOCK
    device_lists = neighbours.reshape(N_SPACE, BLK_DEV, KNB)
    device_ids = jnp.arange(N_SPACE, dtype=jnp.int32)

    def space_setup(frame_in):
        normed = rms_norm(frame_in)
        projected = jnp.dot(normed, w_qkv_space, preferred_element_type=jnp.float32).astype(jnp.bfloat16)
        queries = projected[:, :feature_count].reshape(N_SPACE, shard, feature_count)
        key_window = windows(projected[:, feature_count:2 * feature_count].reshape(N_SPACE, shard, feature_count))
        value_window = windows(projected[:, 2 * feature_count:].reshape(N_SPACE, shard, feature_count))

        def one_device(item):
            query_rows, key_rows, value_rows, lists_here, device_id = item
            allowed = block_mask(lists_here, (device_id - 1) * BLK_DEV)
            return space_attend(query_rows, key_rows, value_rows, allowed)
        attended, totals = lax.map(one_device, (queries, key_window, value_window, device_lists, device_ids))
        return (queries, key_window, value_window, attended, totals)

    def space_forward(frame_in):
        attended = space_setup(frame_in)[3]
        update = jnp.dot(attended.reshape(frame_tokens, feature_count), w_out_space, preferred_element_type=jnp.float32)
        return (frame_in.astype(jnp.float32) + update).astype(jnp.bfloat16)
    stream = lax.map(space_forward, frames_in)
    stream_dev = stream.reshape(frame_count, N_SPACE, shard, feature_count).transpose(1, 0, 2, 3)
    grad_dev = cotangent.reshape(frame_count, N_SPACE, shard, feature_count).transpose(1, 0, 2, 3)

    def time_device(item):
        return time_block(item[0], item[1], w_qkv_time, w_out_time)
    out_dev, stream_grad_dev = lax.map(time_device, (stream_dev, grad_dev))
    frames_out = out_dev.transpose(1, 0, 2, 3).reshape(frame_count, frame_tokens, feature_count)
    grad_stream = stream_grad_dev.transpose(1, 0, 2, 3).reshape(frame_count, frame_tokens, feature_count)

    def space_backward(item):
        frame_in, grad_frame = item
        queries, key_window, value_window, attended, totals = space_setup(frame_in)
        grad_attended = jnp.dot(grad_frame, w_out_space.T, preferred_element_type=jnp.float32)
        grad_attended = grad_attended.astype(jnp.bfloat16).reshape(N_SPACE, shard, feature_count)

        def one_device(parts):
            query_rows, key_rows, value_rows, lists_here, device_id, attended_rows, total_rows, grad_rows = parts
            allowed = block_mask(lists_here, (device_id - 1) * BLK_DEV)
            return space_back(query_rows, key_rows, value_rows, allowed, total_rows, attended_rows, grad_rows)
        grad_query, key_partial, value_partial = lax.map(one_device, (queries, key_window, value_window, device_lists, device_ids, attended, totals, grad_attended))
        grad_key = combine(key_partial, shard)
        grad_value = combine(value_partial, shard)
        grad_project = jnp.concatenate([grad_query, grad_key, grad_value], axis=-1)
        grad_normed = jnp.dot(grad_project.reshape(frame_tokens, 3 * feature_count), w_qkv_space.T, preferred_element_type=jnp.float32)
        return (grad_frame.astype(jnp.float32) + rms_back(frame_in, grad_normed)).astype(jnp.bfloat16)
    grad_frames = lax.map(space_backward, (frames_in, grad_stream))
    return (frames_out, grad_frames)
```

```python
import functools

import jax
import jax.numpy as jnp
from jax import lax
from jax.experimental import pallas as pl
from jax.experimental.pallas import tpu as pltpu
from jax.sharding import PartitionSpec as P

HEADS = 12
HD = 64
D = 768
ROWS = 128
PAIRS = HEADS // 2
EPS = 1e-06
FAR = -1e30
SCALE = HD ** (-0.5)
F32 = jnp.float32
BF16 = jnp.bfloat16
TILE = 256


def dot(a, b):
    return jnp.dot(a, b, preferred_element_type=F32)


def dot_nt(a, b):
    return lax.dot_general(a, b, (((1,), (1,)), ((), ())), preferred_element_type=F32)


def dot_tn(a, b):
    return lax.dot_general(a, b, (((0,), (0,)), ((), ())), preferred_element_type=F32)


def rms_factor(values):
    return lax.rsqrt(jnp.mean(values * values, axis=-1, keepdims=True) + EPS)


def rms_back(values, upstream):
    factor = rms_factor(values)
    inner = jnp.mean(values * upstream, axis=-1, keepdims=True)
    return factor * upstream - values * (factor * factor * factor * inner)


def remote(src, dst, send, recv, where):
    return pltpu.make_async_remote_copy(
        src_ref=src,
        dst_ref=dst,
        send_sem=send,
        recv_sem=recv,
        device_id=where,
        device_id_type=pl.DeviceIdType.MESH,
    )


class Gather:
    X = 2
    Z = 4

    def __init__(self, weights, sems):
        self.w = weights
        self.zs, self.zr, self.xs, self.xr, self.ys, self.yr, self.cs, self.cr = sems
        self.s = lax.axis_index("space")
        self.z = self.s // self.X
        self.x = self.s % self.X
        self.odd = lax.axis_index("frame")
        self.c = lax.axis_index("dp")

    def rows(self, group, shard, offset, count):
        start = pl.multiple_of(shard * 96 + offset, 16)
        return self.w.at[group, pl.ds(start, count), :]

    def main(self, group, shard):
        return self.rows(group, shard, 48 * self.c + 16 * self.odd, 32)

    def along_z(self, group, step, at):
        ref = self.main(group, at * self.X + self.x)
        way = 0 if step > 0 else 1
        return remote(
            ref, ref, self.zs.at[group, way, at], self.zr.at[group, at], {"space": self.s + step * self.X}
        )

    def along_x(self, group, at, column):
        ref = self.main(group, at * self.X + column)
        partner = self.s + 1 - 2 * self.x
        return remote(ref, ref, self.xs.at[group, at], self.xr.at[group, at], {"space": partner})

    def along_y(self, group, shard, sending):
        which = self.odd if sending else 1 - self.odd
        ref = self.rows(group, shard, 48 * self.c + 32 * which, 16)
        return remote(
            ref, ref, self.ys.at[group, shard], self.yr.at[group, shard], {"frame": 1 - self.odd}
        )

    def across(self, group, shard, sending):
        half = self.c if sending else 1 - self.c
        ref = self.rows(group, shard, 48 * half, 48)
        return remote(
            ref, ref, self.cs.at[group, shard], self.cr.at[group, shard], {"dp": 1 - self.c}
        )

    def open(self, group):
        @pl.when(self.z < self.Z - 1)
        def _():
            self.along_z(group, 1, self.z).start()

        @pl.when(self.z > 0)
        def _():
            self.along_z(group, -1, self.z).start()

        self.along_x(group, self.z, self.x).start()

    def z_step(self, group, distance):
        for step in (1, -1):
            at = self.z - step * distance

            @pl.when((at >= 0) & (at < self.Z))
            def _():
                self.along_z(group, -step, at).wait_recv()
                onward = (self.z + step >= 0) & (self.z + step < self.Z)

                @pl.when(onward)
                def _():
                    self.along_z(group, step, at).start()

                self.along_x(group, at, self.x).start()
                self.along_y(group, at * self.X + self.x, True).start()

    def x_step(self, group, distance):
        for step in (1, -1) if distance else (1,):
            at = self.z - step * distance

            @pl.when((at >= 0) & (at < self.Z))
            def _():
                self.along_x(group, at, 1 - self.x).wait_recv()
                self.along_y(group, at * self.X + 1 - self.x, True).start()

    def zx_stage(self, group):
        for distance in range(1, self.Z):
            self.z_step(group, distance)
            self.x_step(group, distance - 1)
        self.x_step(group, self.Z - 1)

    def others(self):
        count = self.X * self.Z
        return [lax.rem(self.s + k, count) for k in range(1, count)]

    def y_stage(self, group):
        for shard in self.others():
            self.along_y(group, shard, False).wait_recv()
            self.across(group, shard, True).start()

    def c_stage(self, group):
        for shard in self.others():
            self.across(group, shard, False).wait_recv()

    def close(self, group):
        for at in range(self.Z):

            @pl.when((self.z < self.Z - 1) & (at <= self.z))
            def _():
                self.along_z(group, 1, at).wait_send()

            @pl.when((self.z > 0) & (at >= self.z))
            def _():
                self.along_z(group, -1, at).wait_send()

            self.along_x(group, at, self.x).wait_send()
        for shard in self.others():
            self.along_y(group, shard, True).wait_send()
            self.across(group, shard, True).wait_send()


def kernel(
    frames, count, gathers,
    x_ref, cot_ref, wqs_ref, wos_ref, wqt_ref, wot_ref, nb_ref,
    out_ref, grad_ref,
    weights, q_buf, kv_win, att, probs, stream, rows_a, big, tsend, tgot, usend, ugot,
    attn_t, grads, gown, gsend, ggot, acc,
    load_sem, zs, zr, xs, xr, ys, yr, cs, cr, hs, hr, bs, br, ts, tr, us, ur,
):
    s = lax.axis_index("space")
    f = lax.axis_index("frame")
    c = lax.axis_index("dp")

    barrier = pltpu.get_barrier_semaphore()
    peers = [{"space": lax.rem(s + k, count)} for k in (1, 2, count - 2, count - 1)]
    peers += [{"frame": lax.rem(f + k, frames)} for k in range(1, frames)]
    peers += [{"dp": 1 - c}]
    for peer in peers:
        pl.semaphore_signal(barrier, inc=1, device_id=peer, device_id_type=pl.DeviceIdType.MESH)

    depth = wqs_ref.shape[0]
    start = pl.multiple_of(s * depth, 16) if gathers else 0
    here = pl.ds(start, depth)
    loads = [
        pltpu.make_async_copy(ref, weights.at[group, here, pl.ds(col, ref.shape[1])], load_sem.at[i])
        for i, (ref, group, col) in enumerate(
            ((wqs_ref, 0, 0), (wos_ref, 0, 3 * D), (wqt_ref, 1, 0), (wot_ref, 1, 3 * D))
        )
    ]
    for load in loads:
        load.start()

    lane = lax.broadcasted_iota(jnp.int32, (1, 2 * HD), 1)
    first = lane < HD
    first_row = first.astype(F32).astype(BF16)
    second_row = (1.0 - first.astype(F32)).astype(BF16)

    def stacked(pair):
        return jnp.concatenate([pair * first_row, pair * second_row], axis=0)

    def joined(both):
        return jnp.where(first, both[:ROWS], both[ROWS:])

    def forward(rows, group, col, width, put):
        def body(i, carry):
            at = pl.multiple_of(i * TILE, TILE)
            put(at, dot(rows[...], weights[group, :, pl.ds(col + at, TILE)]))
            return carry

        lax.fori_loop(0, width // TILE, body, 0)

    def backward(rows, cols, group, put):
        def body(i, carry):
            at = pl.multiple_of(i * TILE, TILE)
            put(at, dot_nt(rows[...], weights[group, pl.ds(at, TILE), cols]))
            return carry

        lax.fori_loop(0, D // TILE, body, 0)

    def into(ref, col=0):
        def put(at, value):
            ref[:, pl.ds(col + at, TILE)] = value.astype(ref.dtype)

        return put

    values = x_ref[...].astype(F32)
    rows_a[...] = (values * rms_factor(values)).astype(BF16)

    @pl.when(s == 0)
    def _():
        kv_win[0:ROWS, :] = jnp.zeros((ROWS, 2 * D), BF16)
        ggot[0] = jnp.zeros((ROWS, 2 * D), BF16)

    @pl.when(s == count - 1)
    def _():
        kv_win[2 * ROWS : 3 * ROWS, :] = jnp.zeros((ROWS, 2 * D), BF16)
        ggot[1] = jnp.zeros((ROWS, 2 * D), BF16)

    for load in loads:
        load.wait()
    pl.semaphore_wait(barrier, len(peers))

    gather = Gather(weights, (zs, zr, xs, xr, ys, yr, cs, cr)) if gathers else None
    if gathers:
        gather.open(0)
        gather.open(1)
        gather.zx_stage(0)
        gather.y_stage(0)
        gather.c_stage(0)

    def put_kv(at, value):
        kv_win[ROWS : 2 * ROWS, pl.ds(at, TILE)] = value.astype(BF16)

    forward(rows_a, 0, D, 2 * D, put_kv)
    mine = kv_win.at[pl.ds(ROWS, ROWS), :]
    halo = [
        remote(mine, kv_win.at[pl.ds(2 * ROWS, ROWS), :], hs.at[0], hr.at[0], {"space": s - 1}),
        remote(mine, kv_win.at[pl.ds(0, ROWS), :], hs.at[1], hr.at[1], {"space": s + 1}),
    ]
    back_halo = [
        remote(gsend.at[0], ggot.at[1], bs.at[0], br.at[0], {"space": s - 1}),
        remote(gsend.at[1], ggot.at[0], bs.at[1], br.at[1], {"space": s + 1}),
    ]
    has = [s > 0, s < count - 1]

    def each_way(action):
        for way in range(2):
            pl.when(has[way])(functools.partial(action, way))

    each_way(lambda way: halo[way].start())
    forward(rows_a, 0, 0, D, into(q_buf))

    if gathers:
        gather.zx_stage(1)

    each_way(lambda way: halo[1 - way].wait_recv())

    def listed(block):
        hit = nb_ref[s, 0] == block
        for j in range(1, nb_ref.shape[1]):
            hit = hit | (nb_ref[s, j] == block)
        return jnp.where(hit, 0.0, FAR).astype(F32)

    key_lane = lax.broadcasted_iota(jnp.int32, (1, 3 * ROWS), 1)
    bias = jnp.where(
        key_lane < ROWS, listed(s - 1), jnp.where(key_lane < 2 * ROWS, listed(s), listed(s + 1))
    )

    def attend(hp, carry):
        cols = pl.ds(pl.multiple_of(hp * 128, 128), 128)
        vcols = pl.ds(pl.multiple_of(D + hp * 128, 128), 128)
        scores = dot_nt(stacked(q_buf[:, cols]), kv_win[:, cols]) * SCALE + bias
        expo = jnp.exp(scores)
        weight = expo / jnp.sum(expo, axis=-1, keepdims=True)
        probs[hp] = weight
        att[:, cols] = joined(dot(weight.astype(BF16), kv_win[:, vcols])).astype(BF16)
        return carry

    lax.fori_loop(0, PAIRS, attend, 0)

    if gathers:
        gather.y_stage(1)

    forward(att, 0, 3 * D, D, into(acc))
    stream[...] = (x_ref[...].astype(F32) + acc[...]).astype(BF16)
    values = stream[...].astype(F32)
    rows_a[...] = (values * rms_factor(values)).astype(BF16)

    if gathers:
        gather.c_stage(1)

    forward(rows_a, 1, D, 2 * D, into(tsend.at[0]))
    forward(rows_a, 1, 0, D, into(tsend.at[1]))
    backward(cot_ref, pl.ds(3 * D, D), 1, into(tsend.at[1], D))

    def to_frame(k):
        return remote(
            tsend.at[(f + k) // frames], tgot.at[f], ts.at[k - 1], tr.at[f], {"frame": lax.rem(f + k, frames)}
        )

    def from_frame(k):
        o = lax.rem(f + k, frames)
        return remote(tsend.at[0], tgot.at[o], ts.at[k - 1], tr.at[o], {"frame": o})

    def pairs_to(k):
        return remote(
            usend.at[k - 1], ugot.at[f], us.at[k - 1], ur.at[f], {"frame": lax.rem(f + k, frames)}
        )

    def pairs_from(k):
        o = lax.rem(f + k, frames)
        return remote(usend.at[k - 1], ugot.at[o], us.at[k - 1], ur.at[o], {"frame": o})

    for k in range(1, frames):
        to_frame(k).start()

    hot = (
        lax.broadcasted_iota(jnp.int32, (D, 128), 0) // HD
        == lax.broadcasted_iota(jnp.int32, (D, 128), 1)
    ).astype(F32).astype(BF16)

    def per_head(product):
        high = product.astype(BF16)
        low = (product - high.astype(F32)).astype(BF16)
        return dot(high, hot) + dot(low, hot)

    def spread(heads):
        return dot_nt(heads, hot)

    query = tsend[1, :, 0:D].astype(F32)
    grad_att = tsend[1, :, D : 2 * D].astype(F32)

    def pair_terms(held):
        key = held[:, 0:D].astype(F32)
        value = held[:, D : 2 * D].astype(F32)
        return per_head(query * key) * SCALE, per_head(grad_att * value)

    score, prob_grad = pair_terms(tsend[0])
    expos = [jnp.exp(score)]
    prob_grads = [prob_grad]
    for k in range(1, frames):
        from_frame(k).wait_recv()
        o = lax.rem(f + k, frames)
        score, prob_grad = pair_terms(tgot[o])
        expos.append(jnp.exp(score + jnp.where(o < f, 0.0, FAR).astype(F32)))
        prob_grads.append(prob_grad)
    total = sum(expos[1:], expos[0])
    shares = [expo / total for expo in expos]
    rounded = [share.astype(BF16) for share in shares]

    def held_at(k):
        return tsend[0] if k == 0 else tgot[lax.rem(f + k, frames)]

    update = spread(rounded[0]) * held_at(0)[:, D : 2 * D].astype(F32)
    for k in range(1, frames):
        update = update + spread(rounded[k]) * held_at(k)[:, D : 2 * D].astype(F32)
    attn_t[...] = update.astype(BF16)
    delta = per_head(grad_att * attn_t[...].astype(F32))
    score_grads = [
        (share * (grad - delta)).astype(BF16) for share, grad in zip(shares, prob_grads)
    ]
    for k in range(1, frames):
        usend[k - 1, :, 0:128] = rounded[k]
        usend[k - 1, :, 128:256] = score_grads[k]
        pairs_to(k).start()

    def put_out(at, value):
        cols = pl.ds(at, TILE)
        out_ref[:, cols] = (stream[:, cols].astype(F32) + value).astype(BF16)

    forward(attn_t, 1, 3 * D, D, put_out)

    update = spread(score_grads[0]) * held_at(0)[:, 0:D].astype(F32)
    for k in range(1, frames):
        update = update + spread(score_grads[k]) * held_at(k)[:, 0:D].astype(F32)
    grads[:, 0:D] = (update * SCALE).astype(BF16)

    key_grad = spread(score_grads[0]) * query
    value_grad = spread(rounded[0]) * grad_att
    for k in range(1, frames):
        pairs_from(k).wait_recv()
        o = lax.rem(f + k, frames)
        key_grad = key_grad + spread(ugot[o, :, 128:256]) * tgot[o, :, 0:D].astype(F32)
        value_grad = value_grad + spread(ugot[o, :, 0:128]) * tgot[o, :, D : 2 * D].astype(F32)
    grads[:, D : 2 * D] = (key_grad * SCALE).astype(BF16)
    grads[:, 2 * D : 3 * D] = value_grad.astype(BF16)

    backward(grads, pl.ds(0, 3 * D), 1, into(acc))
    rows_a[...] = (
        cot_ref[...].astype(F32) + rms_back(stream[...].astype(F32), acc[...])
    ).astype(BF16)

    backward(rows_a, pl.ds(3 * D, D), 0, into(big))

    def attend_back(hp, carry):
        cols = pl.ds(pl.multiple_of(hp * 128, 128), 128)
        vcols = pl.ds(pl.multiple_of(D + hp * 128, 128), 128)
        key = kv_win[:, cols]
        grad_two = stacked(big[:, cols])
        query_two = stacked(q_buf[:, cols])
        weight = probs[hp]
        grad_prob = dot_nt(grad_two, kv_win[:, vcols])
        held = att[:, cols].astype(F32)
        row_delta = jnp.sum(
            grad_two.astype(F32) * jnp.concatenate([held, held], axis=0), axis=-1, keepdims=True
        )
        score_grad = (weight * (grad_prob - row_delta)).astype(BF16)
        grads[:, cols] = (joined(dot(score_grad, key)) * SCALE).astype(BF16)
        key_part = dot_tn(score_grad, query_two) * SCALE
        value_part = dot_tn(weight.astype(BF16), grad_two)
        for part, at in ((key_part, cols), (value_part, vcols)):
            gsend[0, :, at] = part[:ROWS].astype(BF16)
            gown[:, at] = part[ROWS : 2 * ROWS]
            gsend[1, :, at] = part[2 * ROWS :].astype(BF16)
        return carry

    lax.fori_loop(0, PAIRS, attend_back, 0)
    each_way(lambda way: back_halo[way].start())
    backward(grads.at[:, pl.ds(0, D)], pl.ds(0, D), 0, into(acc))
    each_way(lambda way: back_halo[1 - way].wait_recv())
    grads[:, D : 3 * D] = (
        gown[...] + ggot[0].astype(F32) + ggot[1].astype(F32)
    ).astype(BF16)

    def put_more(at, value):
        cols = pl.ds(at, TILE)
        acc[:, cols] = acc[:, cols] + value

    backward(grads.at[:, pl.ds(D, 2 * D)], pl.ds(D, 2 * D), 0, put_more)
    grad_ref[...] = (
        rows_a[...].astype(F32) + rms_back(x_ref[...].astype(F32), acc[...])
    ).astype(BF16)

    each_way(lambda way: halo[way].wait_send())
    each_way(lambda way: back_halo[way].wait_send())
    for k in range(1, frames):
        to_frame(k).wait_send()
        pairs_to(k).wait_send()
    if gathers:
        gather.close(0)
        gather.close(1)


def local(frames, count, frames_in, cotangent, w_qkv_space, w_out_space, w_qkv_time, w_out_time, neighbours):
    gathers = frames == 2 and count == 8 and w_qkv_space.shape[0] == 96
    blocks = [w_qkv_space, w_out_space, w_qkv_time, w_out_time]
    if not gathers:
        blocks = [lax.all_gather(block, "space", axis=0, tiled=True) for block in blocks]
    vmem = pl.BlockSpec(memory_space=pltpu.VMEM)
    hbm = pl.BlockSpec(memory_space=pl.ANY)
    dma = pltpu.SemaphoreType.DMA
    wide = (ROWS, 2 * D)
    out, grad = pl.pallas_call(
        functools.partial(kernel, frames, count, gathers),
        out_shape=[jax.ShapeDtypeStruct((ROWS, D), BF16)] * 2,
        in_specs=[vmem, vmem, hbm, hbm, hbm, hbm, pl.BlockSpec(memory_space=pltpu.SMEM)],
        out_specs=[vmem, vmem],
        scratch_shapes=[
            pltpu.VMEM((2, D, 4 * D), BF16),
            pltpu.VMEM((ROWS, D), BF16),
            pltpu.VMEM((3 * ROWS, 2 * D), BF16),
            pltpu.VMEM((ROWS, D), BF16),
            pltpu.VMEM((PAIRS, 2 * ROWS, 3 * ROWS), F32),
            pltpu.VMEM((ROWS, D), BF16),
            pltpu.VMEM((ROWS, D), BF16),
            pltpu.VMEM((ROWS, D), BF16),
            pltpu.VMEM((2,) + wide, BF16),
            pltpu.VMEM((frames,) + wide, BF16),
            pltpu.VMEM((frames - 1, ROWS, 256), BF16),
            pltpu.VMEM((frames, ROWS, 256), BF16),
            pltpu.VMEM((ROWS, D), BF16),
            pltpu.VMEM((ROWS, 3 * D), BF16),
            pltpu.VMEM(wide, F32),
            pltpu.VMEM((2,) + wide, BF16),
            pltpu.VMEM((2,) + wide, BF16),
            pltpu.VMEM((ROWS, D), F32),
            dma((4,)),
            dma((2, 2, 4)), dma((2, 4)), dma((2, 4)), dma((2, 4)),
            dma((2, 8)), dma((2, 8)), dma((2, 8)), dma((2, 8)),
            dma((2,)), dma((2,)), dma((2,)), dma((2,)),
            dma((frames - 1,)), dma((frames,)), dma((frames - 1,)), dma((frames,)),
        ],
        compiler_params=pltpu.CompilerParams(
            collective_id=0, has_side_effects=True, vmem_limit_bytes=56 * 1024 * 1024
        ),
    )(frames_in[0], cotangent[0], *blocks, neighbours)
    return out[None], grad[None]


def solution(mesh):
    rows = P(("dp", "frame"), "space", None)
    held = P("space", None)
    return jax.shard_map(
        functools.partial(local, mesh.shape["frame"], mesh.shape["space"]),
        mesh=mesh,
        in_specs=(rows, rows, held, held, held, held, P()),
        out_specs=(rows, rows),
        check_vma=False,
    )
```

```python
import functools

import jax
import jax.numpy as jnp
from jax import lax
from jax.experimental import pallas as pl
from jax.experimental.pallas import tpu as pltpu
from jax.sharding import PartitionSpec as P

HEADS = 12
HD = 64
D = 768
ROWS = 128
PAIRS = HEADS // 2
EPS = 1e-06
FAR = -1e30
SCALE = HD ** (-0.5)
F32 = jnp.float32
BF16 = jnp.bfloat16
TILE = 256


def dot(a, b):
    return jnp.dot(a, b, preferred_element_type=F32)


def dot_nt(a, b):
    return lax.dot_general(a, b, (((1,), (1,)), ((), ())), preferred_element_type=F32)


def dot_tn(a, b):
    return lax.dot_general(a, b, (((0,), (0,)), ((), ())), preferred_element_type=F32)


def rms_factor(values):
    return lax.rsqrt(jnp.mean(values * values, axis=-1, keepdims=True) + EPS)


def rms_back(values, upstream):
    factor = rms_factor(values)
    inner = jnp.mean(values * upstream, axis=-1, keepdims=True)
    return factor * upstream - values * (factor * factor * factor * inner)


def remote(src, dst, send, recv, where):
    return pltpu.make_async_remote_copy(
        src_ref=src,
        dst_ref=dst,
        send_sem=send,
        recv_sem=recv,
        device_id=where,
        device_id_type=pl.DeviceIdType.MESH,
    )


class Gather:
    X = 2
    Z = 4

    def __init__(self, weights, sems):
        self.w = weights
        self.zs, self.zr, self.xs, self.xr, self.ys, self.yr, self.cs, self.cr = sems
        self.s = lax.axis_index("space")
        self.z = self.s // self.X
        self.x = self.s % self.X
        self.odd = lax.axis_index("frame")
        self.c = lax.axis_index("dp")

    def rows(self, group, shard, offset, count):
        start = pl.multiple_of(shard * 96 + offset, 16)
        return self.w.at[group, pl.ds(start, count), :]

    def main(self, group, shard):
        return self.rows(group, shard, 48 * self.c + 16 * self.odd, 32)

    def along_z(self, group, step, at):
        ref = self.main(group, at * self.X + self.x)
        way = 0 if step > 0 else 1
        return remote(
            ref, ref, self.zs.at[group, way, at], self.zr.at[group, at], {"space": self.s + step * self.X}
        )

    def along_x(self, group, at, column):
        ref = self.main(group, at * self.X + column)
        partner = self.s + 1 - 2 * self.x
        return remote(ref, ref, self.xs.at[group, at], self.xr.at[group, at], {"space": partner})

    def along_y(self, group, shard, sending):
        which = self.odd if sending else 1 - self.odd
        ref = self.rows(group, shard, 48 * self.c + 32 * which, 16)
        return remote(
            ref, ref, self.ys.at[group, shard], self.yr.at[group, shard], {"frame": 1 - self.odd}
        )

    def across(self, group, shard, sending):
        half = self.c if sending else 1 - self.c
        ref = self.rows(group, shard, 48 * half, 48)
        return remote(
            ref, ref, self.cs.at[group, shard], self.cr.at[group, shard], {"dp": 1 - self.c}
        )

    def open(self, group):
        @pl.when(self.z < self.Z - 1)
        def _():
            self.along_z(group, 1, self.z).start()

        @pl.when(self.z > 0)
        def _():
            self.along_z(group, -1, self.z).start()

        self.along_x(group, self.z, self.x).start()

    def z_step(self, group, distance):
        for step in (1, -1):
            at = self.z - step * distance

            @pl.when((at >= 0) & (at < self.Z))
            def _():
                self.along_z(group, -step, at).wait_recv()
                onward = (self.z + step >= 0) & (self.z + step < self.Z)

                @pl.when(onward)
                def _():
                    self.along_z(group, step, at).start()

                self.along_x(group, at, self.x).start()
                self.along_y(group, at * self.X + self.x, True).start()

    def x_step(self, group, distance):
        for step in (1, -1) if distance else (1,):
            at = self.z - step * distance

            @pl.when((at >= 0) & (at < self.Z))
            def _():
                self.along_x(group, at, 1 - self.x).wait_recv()
                self.along_y(group, at * self.X + 1 - self.x, True).start()

    def others(self):
        count = self.X * self.Z
        return [lax.rem(self.s + k, count) for k in range(1, count)]

    def y_stage(self, group):
        for shard in self.others():
            self.along_y(group, shard, False).wait_recv()
            self.across(group, shard, True).start()

    def c_stage(self, group):
        for shard in self.others():
            self.across(group, shard, False).wait_recv()

    def close(self, group):
        for at in range(self.Z):

            @pl.when((self.z < self.Z - 1) & (at <= self.z))
            def _():
                self.along_z(group, 1, at).wait_send()

            @pl.when((self.z > 0) & (at >= self.z))
            def _():
                self.along_z(group, -1, at).wait_send()

            self.along_x(group, at, self.x).wait_send()
        for shard in self.others():
            self.along_y(group, shard, True).wait_send()
            self.across(group, shard, True).wait_send()


def kernel(
    frames, count, gathers,
    x_ref, cot_ref, wqs_ref, wos_ref, wqt_ref, wot_ref, nb_ref,
    out_ref, grad_ref,
    weights, x_win, normed, qkv, att, probs, near_probs, stream, rows_a, tsend, tgot, usend, ugot,
    attn_t, grads, gown, ga_win, tot, tot_got, dlt, dlt_got, acc,
    load_sem, zs, zr, xs, xr, ys, yr, cs, cr, hs, hr, bs, br, ds, dr, es, er, ts, tr, us, ur,
):
    s = lax.axis_index("space")
    f = lax.axis_index("frame")
    c = lax.axis_index("dp")

    barrier = pltpu.get_barrier_semaphore()
    peers = [{"space": lax.rem(s + k, count)} for k in (1, 2, count - 2, count - 1)]
    peers += [{"frame": lax.rem(f + k, frames)} for k in range(1, frames)]
    peers += [{"dp": 1 - c}]
    for peer in peers:
        pl.semaphore_signal(barrier, inc=1, device_id=peer, device_id_type=pl.DeviceIdType.MESH)

    depth = wqs_ref.shape[0]
    start = pl.multiple_of(s * depth, 16) if gathers else 0
    here = pl.ds(start, depth)
    loads = [
        pltpu.make_async_copy(ref, weights.at[group, here, pl.ds(col, ref.shape[1])], load_sem.at[i])
        for i, (ref, group, col) in enumerate(
            ((wqs_ref, 0, 0), (wos_ref, 0, 3 * D), (wqt_ref, 1, 0), (wot_ref, 1, 3 * D))
        )
    ]
    for load in loads:
        load.start()

    lane = lax.broadcasted_iota(jnp.int32, (1, 2 * HD), 1)
    first = lane < HD
    first_row = first.astype(F32).astype(BF16)
    second_row = (1.0 - first.astype(F32)).astype(BF16)

    def stacked(pair):
        return jnp.concatenate([pair * first_row, pair * second_row], axis=0)

    def joined(both):
        return jnp.where(first, both[:ROWS], both[ROWS:])

    def forward(rows, group, col, width, put):
        def body(i, carry):
            at = pl.multiple_of(i * TILE, TILE)
            put(at, dot(rows[...], weights[group, :, pl.ds(col + at, TILE)]))
            return carry

        lax.fori_loop(0, width // TILE, body, 0)

    def backward(rows, cols, group, put):
        def body(i, carry):
            at = pl.multiple_of(i * TILE, TILE)
            put(at, dot_nt(rows[...], weights[group, pl.ds(at, TILE), cols]))
            return carry

        lax.fori_loop(0, D // TILE, body, 0)

    def into(ref, col=0):
        def put(at, value):
            ref[:, pl.ds(col + at, TILE)] = value.astype(ref.dtype)

        return put

    own = pl.ds(ROWS, ROWS)
    sides = (pl.ds(0, ROWS), pl.ds(2 * ROWS, ROWS))
    has = [s > 0, s < count - 1]

    def two_ways(src, slots, send, recv):
        return [
            remote(src, slots[1 - way], send.at[way], recv.at[way], {"space": s + 2 * way - 1})
            for way in range(2)
        ]

    def each_way(action):
        for way in range(2):
            pl.when(has[way])(functools.partial(action, way))

    def leave(copies):
        each_way(lambda way: copies[way].start())

    def arrive(copies):
        each_way(lambda way: copies[1 - way].wait_recv())

    x_halo = two_ways(x_ref, [x_win.at[side, :] for side in sides], hs, hr)
    ga_halo = two_ways(ga_win.at[own, :], [ga_win.at[side, :] for side in sides], bs, br)
    tot_halo = two_ways(tot, [tot_got.at[way] for way in range(2)], ds, dr)
    dlt_halo = two_ways(dlt, [dlt_got.at[way] for way in range(2)], es, er)

    x_win[own, :] = x_ref[...]
    for way in range(2):

        @pl.when(jnp.logical_not(has[way]))
        def _():
            x_win[sides[way], :] = jnp.zeros((ROWS, D), BF16)
            ga_win[sides[way], :] = jnp.zeros((ROWS, D), BF16)
            tot_got[way] = jnp.ones((ROWS, 128), F32)
            dlt_got[way] = jnp.zeros((ROWS, 128), F32)

    for load in loads:
        load.wait()
    pl.semaphore_wait(barrier, len(peers))

    leave(x_halo)
    gather = Gather(weights, (zs, zr, xs, xr, ys, yr, cs, cr)) if gathers else None

    def pass_on(*steps):
        if gathers:
            for name, *where in steps:
                getattr(gather, name)(*where)

    pass_on(
        ("open", 0), ("open", 1),
        ("z_step", 0, 1), ("x_step", 0, 0), ("z_step", 0, 2), ("x_step", 0, 1), ("z_step", 0, 3),
        ("x_step", 0, 2), ("z_step", 1, 1), ("x_step", 0, 3),
    )
    arrive(x_halo)
    values = x_win[...].astype(F32)
    normed[...] = (values * rms_factor(values)).astype(BF16)
    pass_on(("y_stage", 0), ("z_step", 1, 2), ("x_step", 1, 0), ("c_stage", 0))
    forward(normed, 0, 0, D, into(qkv))
    pass_on(("z_step", 1, 3), ("x_step", 1, 1))
    forward(normed, 0, D, 2 * D, into(qkv, D))
    pass_on(("x_step", 1, 2), ("x_step", 1, 3))

    def listed(block):
        hit = nb_ref[s, 0] == block
        for j in range(1, nb_ref.shape[1]):
            hit = hit | (nb_ref[s, j] == block)
        return jnp.where(hit, 0.0, FAR).astype(F32)

    key_lane = lax.broadcasted_iota(jnp.int32, (1, 3 * ROWS), 1)
    bias = jnp.where(
        key_lane < ROWS, listed(s - 1), jnp.where(key_lane < 2 * ROWS, listed(s), listed(s + 1))
    )

    head_lane = lax.broadcasted_iota(jnp.int32, (1, 128), 1)

    def cols_of(hp, part):
        return pl.ds(pl.multiple_of(part * D + hp * 128, 128), 128)

    def attend(hp, totals):
        cols = cols_of(hp, 0)
        scores = dot_nt(stacked(qkv[own, cols]), qkv[:, cols_of(hp, 1)]) * SCALE + bias
        expo = jnp.exp(scores)
        total = jnp.sum(expo, axis=-1, keepdims=True)
        weight = expo / total
        probs[hp] = weight
        att[:, cols] = joined(dot(weight.astype(BF16), qkv[:, cols_of(hp, 2)])).astype(BF16)
        totals = jnp.where(head_lane == 2 * hp, total[:ROWS], totals)
        return jnp.where(head_lane == 2 * hp + 1, total[ROWS:], totals)

    tot[...] = lax.fori_loop(0, PAIRS, attend, jnp.ones((ROWS, 128), F32))
    leave(tot_halo)

    if gathers:
        gather.y_stage(1)

    forward(att, 0, 3 * D, D, into(acc))
    stream[...] = (x_ref[...].astype(F32) + acc[...]).astype(BF16)
    values = stream[...].astype(F32)
    rows_a[...] = (values * rms_factor(values)).astype(BF16)

    if gathers:
        gather.c_stage(1)

    def frame_copy(k, half, o, slot):
        cols = pl.ds(half * D, D)
        return remote(
            tsend.at[(f + k) // frames, :, cols], tgot.at[slot, :, cols],
            ts.at[k - 1, half], tr.at[slot, half], {"frame": o},
        )

    def to_frame(k, half):
        return frame_copy(k, half, lax.rem(f + k, frames), f)

    def from_frame(k, half):
        o = lax.rem(f + k, frames)
        return frame_copy(k, half, o, o)

    def to_later(half):
        for k in range(1, frames):
            pl.when(f + k < frames)(lambda: to_frame(k, half).start())

    def to_earlier(half):
        for k in range(1, frames):
            pl.when(f + k >= frames)(lambda: to_frame(k, half).start())

    forward(rows_a, 1, D, D, into(tsend.at[0]))
    to_later(0)
    forward(rows_a, 1, 2 * D, D, into(tsend.at[0], D))
    to_later(1)
    forward(rows_a, 1, 0, D, into(tsend.at[1]))
    to_earlier(0)
    backward(cot_ref, pl.ds(3 * D, D), 1, into(tsend.at[1], D))
    to_earlier(1)

    def listed_by(block):
        row = jnp.clip(block, 0, count - 1)
        hit = nb_ref[row, 0] == s
        for j in range(1, nb_ref.shape[1]):
            hit = hit | (nb_ref[row, j] == s)
        return jnp.where(hit & (block >= 0) & (block < count), 0.0, FAR).astype(F32)

    def both_sides(window, cols):
        return jnp.concatenate([stacked(window[side, cols]) for side in sides], axis=0)

    def column(held, hp):
        return [
            jnp.sum(jnp.where(head_lane == 2 * hp + i, held, 0.0), axis=-1, keepdims=True)
            for i in range(2)
        ]

    near_row = lax.broadcasted_iota(jnp.int32, (4 * ROWS, 1), 0)
    near_bias = jnp.where(near_row < 2 * ROWS, listed_by(s - 1), listed_by(s + 1))

    def near(hp, carry):
        query_four = both_sides(qkv, cols_of(hp, 0))
        scores = dot_nt(query_four, qkv[own, cols_of(hp, 1)]) * SCALE + near_bias
        totals = jnp.concatenate(column(tot_got[0], hp) + column(tot_got[1], hp), axis=0)
        near_probs[hp] = jnp.exp(scores) / totals
        return carry

    arrive(tot_halo)
    lax.fori_loop(0, PAIRS, near, 0)

    def pairs_to(k):
        return remote(
            usend.at[k - 1], ugot.at[f], us.at[k - 1], ur.at[f], {"frame": lax.rem(f + k, frames)}
        )

    def pairs_from(k):
        o = lax.rem(f + k, frames)
        return remote(usend.at[k - 1], ugot.at[o], us.at[k - 1], ur.at[o], {"frame": o})

    hot = (
        lax.broadcasted_iota(jnp.int32, (D, 128), 0) // HD
        == lax.broadcasted_iota(jnp.int32, (D, 128), 1)
    ).astype(F32).astype(BF16)

    def per_head(product):
        high = product.astype(BF16)
        low = (product - high.astype(F32)).astype(BF16)
        return dot(high, hot) + dot(low, hot)

    def spread(heads):
        return dot_nt(heads, hot)

    query = tsend[1, :, 0:D].astype(F32)
    grad_att = tsend[1, :, D : 2 * D].astype(F32)

    def pair_terms(held):
        key = held[:, 0:D].astype(F32)
        value = held[:, D : 2 * D].astype(F32)
        return per_head(query * key) * SCALE, per_head(grad_att * value)

    score, prob_grad = pair_terms(tsend[0])
    expos = [jnp.exp(score)]
    prob_grads = [prob_grad]
    for k in range(1, frames):
        from_frame(k, 0).wait_recv()
        from_frame(k, 1).wait_recv()
        o = lax.rem(f + k, frames)
        score, prob_grad = pair_terms(tgot[o])
        expos.append(jnp.exp(score + jnp.where(o < f, 0.0, FAR).astype(F32)))
        prob_grads.append(prob_grad)
    total = sum(expos[1:], expos[0])
    shares = [expo / total for expo in expos]
    rounded = [share.astype(BF16) for share in shares]

    def held_at(k):
        return tsend[0] if k == 0 else tgot[lax.rem(f + k, frames)]

    update = spread(rounded[0]) * held_at(0)[:, D : 2 * D].astype(F32)
    for k in range(1, frames):
        update = update + spread(rounded[k]) * held_at(k)[:, D : 2 * D].astype(F32)
    attn_t[...] = update.astype(BF16)
    delta = per_head(grad_att * attn_t[...].astype(F32))
    score_grads = [
        (share * (grad - delta)).astype(BF16) for share, grad in zip(shares, prob_grads)
    ]
    for k in range(1, frames):
        usend[k - 1, :, 0:128] = rounded[k]
        usend[k - 1, :, 128:256] = score_grads[k]
        pairs_to(k).start()

    def put_out(at, value):
        cols = pl.ds(at, TILE)
        out_ref[:, cols] = (stream[:, cols].astype(F32) + value).astype(BF16)

    forward(attn_t, 1, 3 * D, D, put_out)

    update = spread(score_grads[0]) * held_at(0)[:, 0:D].astype(F32)
    for k in range(1, frames):
        update = update + spread(score_grads[k]) * held_at(k)[:, 0:D].astype(F32)
    grads[:, 0:D] = (update * SCALE).astype(BF16)

    key_grad = spread(score_grads[0]) * query
    value_grad = spread(rounded[0]) * grad_att
    for k in range(1, frames):
        pairs_from(k).wait_recv()
        o = lax.rem(f + k, frames)
        key_grad = key_grad + spread(ugot[o, :, 128:256]) * tgot[o, :, 0:D].astype(F32)
        value_grad = value_grad + spread(ugot[o, :, 0:128]) * tgot[o, :, D : 2 * D].astype(F32)
    grads[:, D : 2 * D] = (key_grad * SCALE).astype(BF16)
    grads[:, 2 * D : 3 * D] = value_grad.astype(BF16)

    backward(grads, pl.ds(0, 3 * D), 1, into(acc))
    rows_a[...] = (
        cot_ref[...].astype(F32) + rms_back(stream[...].astype(F32), acc[...])
    ).astype(BF16)

    def put_ga(at, value):
        ga_win[own, pl.ds(at, TILE)] = value.astype(BF16)

    backward(rows_a, pl.ds(3 * D, D), 0, put_ga)
    leave(ga_halo)
    dlt[...] = per_head(ga_win[own, :].astype(F32) * att[...].astype(F32))
    leave(dlt_halo)

    def attend_back(hp, carry):
        cols = cols_of(hp, 0)
        grad_two = stacked(ga_win[own, cols])
        weight = probs[hp]
        grad_prob = dot_nt(grad_two, qkv[:, cols_of(hp, 2)])
        row_delta = jnp.concatenate(column(dlt[...], hp), axis=0)
        score_grad = (weight * (grad_prob - row_delta)).astype(BF16)
        grads[:, cols] = (joined(dot(score_grad, qkv[:, cols_of(hp, 1)])) * SCALE).astype(BF16)
        middle = slice(ROWS, 2 * ROWS)
        gown[:, cols] = dot_tn(score_grad[:, middle], stacked(qkv[own, cols]))
        gown[:, cols_of(hp, 1)] = dot_tn(weight[:, middle].astype(BF16), grad_two)
        return carry

    lax.fori_loop(0, PAIRS, attend_back, 0)
    backward(grads.at[:, pl.ds(0, D)], pl.ds(0, D), 0, into(acc))
    arrive(ga_halo)
    arrive(dlt_halo)

    def near_back(hp, carry):
        cols = cols_of(hp, 0)
        grad_four = both_sides(ga_win, cols)
        weight = near_probs[hp]
        grad_prob = dot_nt(grad_four, qkv[own, cols_of(hp, 2)])
        row_delta = jnp.concatenate(column(dlt_got[0], hp) + column(dlt_got[1], hp), axis=0)
        score_grad = (weight * (grad_prob - row_delta)).astype(BF16)
        key_grad = gown[:, cols] + dot_tn(score_grad, both_sides(qkv, cols))
        value_grad = gown[:, cols_of(hp, 1)] + dot_tn(weight.astype(BF16), grad_four)
        grads[:, cols_of(hp, 1)] = (key_grad * SCALE).astype(BF16)
        grads[:, cols_of(hp, 2)] = value_grad.astype(BF16)
        return carry

    lax.fori_loop(0, PAIRS, near_back, 0)

    def put_more(at, value):
        cols = pl.ds(at, TILE)
        acc[:, cols] = acc[:, cols] + value

    backward(grads.at[:, pl.ds(D, 2 * D)], pl.ds(D, 2 * D), 0, put_more)
    grad_ref[...] = (
        rows_a[...].astype(F32) + rms_back(x_ref[...].astype(F32), acc[...])
    ).astype(BF16)

    for copies in (x_halo, tot_halo, ga_halo, dlt_halo):
        each_way(lambda way: copies[way].wait_send())
    for k in range(1, frames):
        for half in range(2):
            to_frame(k, half).wait_send()
        pairs_to(k).wait_send()
    if gathers:
        gather.close(0)
        gather.close(1)


def local(frames, count, frames_in, cotangent, w_qkv_space, w_out_space, w_qkv_time, w_out_time, neighbours):
    gathers = frames == 2 and count == 8 and w_qkv_space.shape[0] == 96
    blocks = [w_qkv_space, w_out_space, w_qkv_time, w_out_time]
    if not gathers:
        blocks = [lax.all_gather(block, "space", axis=0, tiled=True) for block in blocks]
    vmem = pl.BlockSpec(memory_space=pltpu.VMEM)
    hbm = pl.BlockSpec(memory_space=pl.ANY)
    dma = pltpu.SemaphoreType.DMA
    wide = (ROWS, 2 * D)
    out, grad = pl.pallas_call(
        functools.partial(kernel, frames, count, gathers),
        out_shape=[jax.ShapeDtypeStruct((ROWS, D), BF16)] * 2,
        in_specs=[vmem, vmem, hbm, hbm, hbm, hbm, pl.BlockSpec(memory_space=pltpu.SMEM)],
        out_specs=[vmem, vmem],
        scratch_shapes=[
            pltpu.VMEM((2, D, 4 * D), BF16),
            pltpu.VMEM((3 * ROWS, D), BF16),
            pltpu.VMEM((3 * ROWS, D), BF16),
            pltpu.VMEM((3 * ROWS, 3 * D), BF16),
            pltpu.VMEM((ROWS, D), BF16),
            pltpu.VMEM((PAIRS, 2 * ROWS, 3 * ROWS), F32),
            pltpu.VMEM((PAIRS, 4 * ROWS, ROWS), F32),
            pltpu.VMEM((ROWS, D), BF16),
            pltpu.VMEM((ROWS, D), BF16),
            pltpu.VMEM((2,) + wide, BF16),
            pltpu.VMEM((frames,) + wide, BF16),
            pltpu.VMEM((frames - 1, ROWS, 256), BF16),
            pltpu.VMEM((frames, ROWS, 256), BF16),
            pltpu.VMEM((ROWS, D), BF16),
            pltpu.VMEM((ROWS, 3 * D), BF16),
            pltpu.VMEM(wide, F32),
            pltpu.VMEM((3 * ROWS, D), BF16),
            pltpu.VMEM((ROWS, 128), F32),
            pltpu.VMEM((2, ROWS, 128), F32),
            pltpu.VMEM((ROWS, 128), F32),
            pltpu.VMEM((2, ROWS, 128), F32),
            pltpu.VMEM((ROWS, D), F32),
            dma((4,)),
            dma((2, 2, 4)), dma((2, 4)), dma((2, 4)), dma((2, 4)),
            dma((2, 8)), dma((2, 8)), dma((2, 8)), dma((2, 8)),
            *[dma((2,))] * 8,
            dma((frames - 1, 2)), dma((frames, 2)), dma((frames - 1,)), dma((frames,)),
        ],
        compiler_params=pltpu.CompilerParams(
            collective_id=0, has_side_effects=True, vmem_limit_bytes=56 * 1024 * 1024
        ),
    )(frames_in[0], cotangent[0], *blocks, neighbours)
    return out[None], grad[None]


def solution(mesh):
    rows = P(("dp", "frame"), "space", None)
    held = P("space", None)
    return jax.shard_map(
        functools.partial(local, mesh.shape["frame"], mesh.shape["space"]),
        mesh=mesh,
        in_specs=(rows, rows, held, held, held, held, P()),
        out_specs=(rows, rows),
        check_vma=False,
    )
```

```python
import functools

import jax
import jax.numpy as jnp
from jax import lax
from jax.experimental import pallas as pl
from jax.experimental.pallas import tpu as pltpu
from jax.sharding import PartitionSpec as P

HEADS = 12
HD = 64
D = 768
ROWS = 128
PAIRS = HEADS // 2
EPS = 1e-06
FAR = -1e30
SCALE = HD ** (-0.5)
F32 = jnp.float32
BF16 = jnp.bfloat16
TILE = 256


def dot(a, b):
    return jnp.dot(a, b, preferred_element_type=F32)


def dot_nt(a, b):
    return lax.dot_general(a, b, (((1,), (1,)), ((), ())), preferred_element_type=F32)


def dot_tn(a, b):
    return lax.dot_general(a, b, (((0,), (0,)), ((), ())), preferred_element_type=F32)


def rms_factor(values):
    return lax.rsqrt(jnp.mean(values * values, axis=-1, keepdims=True) + EPS)


def rms_back(values, upstream):
    factor = rms_factor(values)
    inner = jnp.mean(values * upstream, axis=-1, keepdims=True)
    return factor * upstream - values * (factor * factor * factor * inner)


def remote(src, dst, send, recv, where):
    return pltpu.make_async_remote_copy(
        src_ref=src,
        dst_ref=dst,
        send_sem=send,
        recv_sem=recv,
        device_id=where,
        device_id_type=pl.DeviceIdType.MESH,
    )


class Gather:
    X = 2
    Z = 4

    def __init__(self, weights, sems):
        self.w = weights
        self.zs, self.zr, self.xs, self.xr, self.ys, self.yr, self.cs, self.cr = sems
        self.s = lax.axis_index("space")
        self.z = self.s // self.X
        self.x = self.s % self.X
        self.odd = lax.axis_index("frame")
        self.c = lax.axis_index("dp")

    def rows(self, group, shard, offset, count):
        start = pl.multiple_of(shard * 96 + offset, 16)
        return self.w.at[group, pl.ds(start, count), :]

    def main(self, group, shard):
        return self.rows(group, shard, 48 * self.c + 16 * self.odd, 32)

    def along_z(self, group, step, at):
        ref = self.main(group, at * self.X + self.x)
        way = 0 if step > 0 else 1
        return remote(
            ref, ref, self.zs.at[group, way, at], self.zr.at[group, at], {"space": self.s + step * self.X}
        )

    def along_x(self, group, at, column):
        ref = self.main(group, at * self.X + column)
        partner = self.s + 1 - 2 * self.x
        return remote(ref, ref, self.xs.at[group, at], self.xr.at[group, at], {"space": partner})

    def along_y(self, group, shard, sending):
        which = self.odd if sending else 1 - self.odd
        ref = self.rows(group, shard, 48 * self.c + 32 * which, 16)
        return remote(
            ref, ref, self.ys.at[group, shard], self.yr.at[group, shard], {"frame": 1 - self.odd}
        )

    def across(self, group, shard, sending):
        half = self.c if sending else 1 - self.c
        ref = self.rows(group, shard, 48 * half, 48)
        return remote(
            ref, ref, self.cs.at[group, shard], self.cr.at[group, shard], {"dp": 1 - self.c}
        )

    def open(self, group):
        @pl.when(self.z < self.Z - 1)
        def _():
            self.along_z(group, 1, self.z).start()

        @pl.when(self.z > 0)
        def _():
            self.along_z(group, -1, self.z).start()

        self.along_x(group, self.z, self.x).start()

    def z_step(self, group, distance):
        for step in (1, -1):
            at = self.z - step * distance

            @pl.when((at >= 0) & (at < self.Z))
            def _():
                self.along_z(group, -step, at).wait_recv()
                onward = (self.z + step >= 0) & (self.z + step < self.Z)

                @pl.when(onward)
                def _():
                    self.along_z(group, step, at).start()

                self.along_x(group, at, self.x).start()
                self.along_y(group, at * self.X + self.x, True).start()

    def x_step(self, group, distance):
        for step in (1, -1) if distance else (1,):
            at = self.z - step * distance

            @pl.when((at >= 0) & (at < self.Z))
            def _():
                self.along_x(group, at, 1 - self.x).wait_recv()
                self.along_y(group, at * self.X + 1 - self.x, True).start()

    def others(self):
        count = self.X * self.Z
        return [lax.rem(self.s + k, count) for k in range(1, count)]

    def y_stage(self, group):
        for shard in self.others():
            self.along_y(group, shard, False).wait_recv()
            self.across(group, shard, True).start()

    def c_stage(self, group):
        for shard in self.others():
            self.across(group, shard, False).wait_recv()

    def close(self, group):
        for at in range(self.Z):

            @pl.when((self.z < self.Z - 1) & (at <= self.z))
            def _():
                self.along_z(group, 1, at).wait_send()

            @pl.when((self.z > 0) & (at >= self.z))
            def _():
                self.along_z(group, -1, at).wait_send()

            self.along_x(group, at, self.x).wait_send()
        for shard in self.others():
            self.along_y(group, shard, True).wait_send()
            self.across(group, shard, True).wait_send()


def kernel(
    frames, count, gathers,
    x_ref, cot_ref, wqs_ref, wos_ref, wqt_ref, wot_ref, nb_ref,
    out_ref, grad_ref,
    weights, x_win, normed, qkv, att, probs, near_probs, stream, rows_a, tsend, tgot, usend, ugot,
    attn_t, grads, gown, ga_win, tot, tot_got, dlt, dlt_got, acc,
    load_sem, zs, zr, xs, xr, ys, yr, cs, cr, hs, hr, bs, br, ds, dr, es, er, ts, tr, us, ur,
):
    s = lax.axis_index("space")
    f = lax.axis_index("frame")
    c = lax.axis_index("dp")

    barrier = pltpu.get_barrier_semaphore()
    peers = [{"space": lax.rem(s + k, count)} for k in (1, 2, count - 2, count - 1)]
    peers += [{"frame": lax.rem(f + k, frames)} for k in range(1, frames)]
    peers += [{"dp": 1 - c}]
    for peer in peers:
        pl.semaphore_signal(barrier, inc=1, device_id=peer, device_id_type=pl.DeviceIdType.MESH)

    depth = wqs_ref.shape[0]
    start = pl.multiple_of(s * depth, 16) if gathers else 0
    here = pl.ds(start, depth)
    loads = [
        pltpu.make_async_copy(ref, weights.at[group, here, pl.ds(col, ref.shape[1])], load_sem.at[i])
        for i, (ref, group, col) in enumerate(
            ((wqs_ref, 0, 0), (wos_ref, 0, 3 * D), (wqt_ref, 1, 0), (wot_ref, 1, 3 * D))
        )
    ]
    for load in loads:
        load.start()

    lane = lax.broadcasted_iota(jnp.int32, (1, 2 * HD), 1)
    first = lane < HD
    first_row = first.astype(F32).astype(BF16)
    second_row = (1.0 - first.astype(F32)).astype(BF16)

    def stacked(pair):
        return jnp.concatenate([pair * first_row, pair * second_row], axis=0)

    def joined(both):
        return jnp.where(first, both[:ROWS], both[ROWS:])

    def forward(rows, group, col, width, put):
        for at in range(0, width, TILE):
            put(at, dot(rows[...], weights[group, :, pl.ds(col + at, TILE)]))

    def backward(rows, cols, group, put):
        for at in range(0, D, TILE):
            put(at, dot_nt(rows[...], weights[group, pl.ds(at, TILE), cols]))

    def into(ref, col=0):
        def put(at, value):
            ref[:, pl.ds(col + at, TILE)] = value.astype(ref.dtype)

        return put

    own = pl.ds(ROWS, ROWS)
    sides = (pl.ds(0, ROWS), pl.ds(2 * ROWS, ROWS))
    has = [s > 0, s < count - 1]

    def two_ways(src, slots, send, recv):
        return [
            remote(src, slots[1 - way], send.at[way], recv.at[way], {"space": s + 2 * way - 1})
            for way in range(2)
        ]

    def each_way(action):
        for way in range(2):
            pl.when(has[way])(functools.partial(action, way))

    def leave(copies):
        each_way(lambda way: copies[way].start())

    def arrive(copies):
        each_way(lambda way: copies[1 - way].wait_recv())

    x_halo = two_ways(x_ref, [x_win.at[side, :] for side in sides], hs, hr)
    ga_halo = two_ways(ga_win.at[own, :], [ga_win.at[side, :] for side in sides], bs, br)
    tot_halo = two_ways(tot, [tot_got.at[way] for way in range(2)], ds, dr)
    dlt_halo = two_ways(dlt, [dlt_got.at[way] for way in range(2)], es, er)

    x_win[own, :] = x_ref[...]
    for way in range(2):

        @pl.when(jnp.logical_not(has[way]))
        def _():
            x_win[sides[way], :] = jnp.zeros((ROWS, D), BF16)
            ga_win[sides[way], :] = jnp.zeros((ROWS, D), BF16)
            tot_got[way] = jnp.ones((ROWS, 128), F32)
            dlt_got[way] = jnp.zeros((ROWS, 128), F32)

    pl.semaphore_wait(barrier, len(peers))
    leave(x_halo)
    for load in loads:
        load.wait()
    gather = Gather(weights, (zs, zr, xs, xr, ys, yr, cs, cr)) if gathers else None

    def pass_on(*steps):
        if gathers:
            for name, *where in steps:
                getattr(gather, name)(*where)

    pass_on(
        ("open", 0), ("open", 1),
        ("z_step", 0, 1), ("x_step", 0, 0), ("z_step", 0, 2), ("x_step", 0, 1), ("z_step", 0, 3),
        ("x_step", 0, 2), ("z_step", 1, 1), ("x_step", 0, 3),
    )
    arrive(x_halo)
    values = x_win[...].astype(F32)
    normed[...] = (values * rms_factor(values)).astype(BF16)
    pass_on(("y_stage", 0), ("z_step", 1, 2), ("x_step", 1, 0), ("c_stage", 0))
    forward(normed, 0, 0, D, into(qkv))
    pass_on(("z_step", 1, 3), ("x_step", 1, 1))
    forward(normed, 0, D, 2 * D, into(qkv, D))
    pass_on(("x_step", 1, 2), ("x_step", 1, 3))

    def listed(block):
        hit = nb_ref[s, 0] == block
        for j in range(1, nb_ref.shape[1]):
            hit = hit | (nb_ref[s, j] == block)
        return jnp.where(hit, 0.0, FAR).astype(F32)

    key_lane = lax.broadcasted_iota(jnp.int32, (1, 3 * ROWS), 1)
    bias = jnp.where(
        key_lane < ROWS, listed(s - 1), jnp.where(key_lane < 2 * ROWS, listed(s), listed(s + 1))
    )

    head_lane = lax.broadcasted_iota(jnp.int32, (1, 128), 1)

    def cols_of(hp, part):
        return pl.ds(part * D + hp * 128, 128)

    def attend(hp, totals):
        cols = cols_of(hp, 0)
        scores = dot_nt(stacked(qkv[own, cols]), qkv[:, cols_of(hp, 1)]) * SCALE + bias
        expo = jnp.exp(scores)
        total = jnp.sum(expo, axis=-1, keepdims=True)
        weight = expo / total
        probs[hp] = weight
        att[:, cols] = joined(dot(weight.astype(BF16), qkv[:, cols_of(hp, 2)])).astype(BF16)
        totals = jnp.where(head_lane == 2 * hp, total[:ROWS], totals)
        return jnp.where(head_lane == 2 * hp + 1, total[ROWS:], totals)

    totals = jnp.ones((ROWS, 128), F32)
    for hp in range(PAIRS):
        totals = attend(hp, totals)
    tot[...] = totals
    leave(tot_halo)

    if gathers:
        gather.y_stage(1)

    forward(att, 0, 3 * D, D, into(acc))
    stream[...] = (x_ref[...].astype(F32) + acc[...]).astype(BF16)
    values = stream[...].astype(F32)
    rows_a[...] = (values * rms_factor(values)).astype(BF16)

    if gathers:
        gather.c_stage(1)

    def frame_copy(k, half, o, slot):
        cols = pl.ds(half * D, D)
        return remote(
            tsend.at[(f + k) // frames, :, cols], tgot.at[slot, :, cols],
            ts.at[k - 1, half], tr.at[slot, half], {"frame": o},
        )

    def to_frame(k, half):
        return frame_copy(k, half, lax.rem(f + k, frames), f)

    def from_frame(k, half):
        o = lax.rem(f + k, frames)
        return frame_copy(k, half, o, o)

    def to_later(half):
        for k in range(1, frames):
            pl.when(f + k < frames)(lambda: to_frame(k, half).start())

    def to_earlier(half):
        for k in range(1, frames):
            pl.when(f + k >= frames)(lambda: to_frame(k, half).start())

    forward(rows_a, 1, D, D, into(tsend.at[0]))
    to_later(0)
    forward(rows_a, 1, 2 * D, D, into(tsend.at[0], D))
    to_later(1)
    forward(rows_a, 1, 0, D, into(tsend.at[1]))
    to_earlier(0)
    backward(cot_ref, pl.ds(3 * D, D), 1, into(tsend.at[1], D))
    to_earlier(1)

    def listed_by(block):
        row = jnp.clip(block, 0, count - 1)
        hit = nb_ref[row, 0] == s
        for j in range(1, nb_ref.shape[1]):
            hit = hit | (nb_ref[row, j] == s)
        return jnp.where(hit & (block >= 0) & (block < count), 0.0, FAR).astype(F32)

    def both_sides(window, cols):
        return jnp.concatenate([stacked(window[side, cols]) for side in sides], axis=0)

    def column(held, hp):
        return [
            jnp.sum(jnp.where(head_lane == 2 * hp + i, held, 0.0), axis=-1, keepdims=True)
            for i in range(2)
        ]

    near_row = lax.broadcasted_iota(jnp.int32, (4 * ROWS, 1), 0)
    near_bias = jnp.where(near_row < 2 * ROWS, listed_by(s - 1), listed_by(s + 1))

    def near(hp):
        query_four = both_sides(qkv, cols_of(hp, 0))
        scores = dot_nt(query_four, qkv[own, cols_of(hp, 1)]) * SCALE + near_bias
        totals = jnp.concatenate(column(tot_got[0], hp) + column(tot_got[1], hp), axis=0)
        near_probs[hp] = jnp.exp(scores) / totals

    arrive(tot_halo)
    for hp in range(PAIRS):
        near(hp)

    def pairs_to(k):
        return remote(
            usend.at[k - 1], ugot.at[f], us.at[k - 1], ur.at[f], {"frame": lax.rem(f + k, frames)}
        )

    def pairs_from(k):
        o = lax.rem(f + k, frames)
        return remote(usend.at[k - 1], ugot.at[o], us.at[k - 1], ur.at[o], {"frame": o})

    hot = (
        lax.broadcasted_iota(jnp.int32, (D, 128), 0) // HD
        == lax.broadcasted_iota(jnp.int32, (D, 128), 1)
    ).astype(F32).astype(BF16)

    def per_head(product):
        high = product.astype(BF16)
        low = (product - high.astype(F32)).astype(BF16)
        return dot(high, hot) + dot(low, hot)

    def spread(heads):
        return dot_nt(heads, hot)

    query = tsend[1, :, 0:D].astype(F32)
    grad_att = tsend[1, :, D : 2 * D].astype(F32)

    def pair_terms(held):
        key = held[:, 0:D].astype(F32)
        value = held[:, D : 2 * D].astype(F32)
        return per_head(query * key) * SCALE, per_head(grad_att * value)

    score, prob_grad = pair_terms(tsend[0])
    expos = [jnp.exp(score)]
    prob_grads = [prob_grad]
    for k in range(1, frames):
        from_frame(k, 0).wait_recv()
        from_frame(k, 1).wait_recv()
        o = lax.rem(f + k, frames)
        score, prob_grad = pair_terms(tgot[o])
        expos.append(jnp.exp(score + jnp.where(o < f, 0.0, FAR).astype(F32)))
        prob_grads.append(prob_grad)
    total = sum(expos[1:], expos[0])
    shares = [expo / total for expo in expos]
    rounded = [share.astype(BF16) for share in shares]

    def held_at(k):
        return tsend[0] if k == 0 else tgot[lax.rem(f + k, frames)]

    update = spread(rounded[0]) * held_at(0)[:, D : 2 * D].astype(F32)
    for k in range(1, frames):
        update = update + spread(rounded[k]) * held_at(k)[:, D : 2 * D].astype(F32)
    attn_t[...] = update.astype(BF16)
    delta = per_head(grad_att * attn_t[...].astype(F32))
    score_grads = [
        (share * (grad - delta)).astype(BF16) for share, grad in zip(shares, prob_grads)
    ]
    for k in range(1, frames):
        usend[k - 1, :, 0:128] = rounded[k]
        usend[k - 1, :, 128:256] = score_grads[k]
        pairs_to(k).start()

    def put_out(at, value):
        cols = pl.ds(at, TILE)
        out_ref[:, cols] = (stream[:, cols].astype(F32) + value).astype(BF16)

    forward(attn_t, 1, 3 * D, D, put_out)

    update = spread(score_grads[0]) * held_at(0)[:, 0:D].astype(F32)
    for k in range(1, frames):
        update = update + spread(score_grads[k]) * held_at(k)[:, 0:D].astype(F32)
    grads[:, 0:D] = (update * SCALE).astype(BF16)

    key_grad = spread(score_grads[0]) * query
    value_grad = spread(rounded[0]) * grad_att
    for k in range(1, frames):
        pairs_from(k).wait_recv()
        o = lax.rem(f + k, frames)
        key_grad = key_grad + spread(ugot[o, :, 128:256]) * tgot[o, :, 0:D].astype(F32)
        value_grad = value_grad + spread(ugot[o, :, 0:128]) * tgot[o, :, D : 2 * D].astype(F32)
    grads[:, D : 2 * D] = (key_grad * SCALE).astype(BF16)
    grads[:, 2 * D : 3 * D] = value_grad.astype(BF16)

    backward(grads, pl.ds(0, 3 * D), 1, into(acc))
    rows_a[...] = (
        cot_ref[...].astype(F32) + rms_back(stream[...].astype(F32), acc[...])
    ).astype(BF16)

    def put_ga(at, value):
        ga_win[own, pl.ds(at, TILE)] = value.astype(BF16)

    backward(rows_a, pl.ds(3 * D, D), 0, put_ga)
    leave(ga_halo)
    dlt[...] = per_head(ga_win[own, :].astype(F32) * att[...].astype(F32))
    leave(dlt_halo)

    def attend_back(hp):
        cols = cols_of(hp, 0)
        grad_two = stacked(ga_win[own, cols])
        weight = probs[hp]
        grad_prob = dot_nt(grad_two, qkv[:, cols_of(hp, 2)])
        row_delta = jnp.concatenate(column(dlt[...], hp), axis=0)
        score_grad = (weight * (grad_prob - row_delta)).astype(BF16)
        grads[:, cols] = (joined(dot(score_grad, qkv[:, cols_of(hp, 1)])) * SCALE).astype(BF16)
        middle = slice(ROWS, 2 * ROWS)
        gown[:, cols] = dot_tn(score_grad[:, middle], stacked(qkv[own, cols]))
        gown[:, cols_of(hp, 1)] = dot_tn(weight[:, middle].astype(BF16), grad_two)

    for hp in range(PAIRS):
        attend_back(hp)
    backward(grads.at[:, pl.ds(0, D)], pl.ds(0, D), 0, into(acc))
    arrive(ga_halo)
    arrive(dlt_halo)

    def near_back(hp):
        cols = cols_of(hp, 0)
        grad_four = both_sides(ga_win, cols)
        weight = near_probs[hp]
        grad_prob = dot_nt(grad_four, qkv[own, cols_of(hp, 2)])
        row_delta = jnp.concatenate(column(dlt_got[0], hp) + column(dlt_got[1], hp), axis=0)
        score_grad = (weight * (grad_prob - row_delta)).astype(BF16)
        key_grad = gown[:, cols] + dot_tn(score_grad, both_sides(qkv, cols))
        value_grad = gown[:, cols_of(hp, 1)] + dot_tn(weight.astype(BF16), grad_four)
        grads[:, cols_of(hp, 1)] = (key_grad * SCALE).astype(BF16)
        grads[:, cols_of(hp, 2)] = value_grad.astype(BF16)

    for hp in range(PAIRS):
        near_back(hp)

    def put_more(at, value):
        cols = pl.ds(at, TILE)
        acc[:, cols] = acc[:, cols] + value

    backward(grads.at[:, pl.ds(D, 2 * D)], pl.ds(D, 2 * D), 0, put_more)
    grad_ref[...] = (
        rows_a[...].astype(F32) + rms_back(x_ref[...].astype(F32), acc[...])
    ).astype(BF16)

    for copies in (x_halo, tot_halo, ga_halo, dlt_halo):
        each_way(lambda way: copies[way].wait_send())
    for k in range(1, frames):
        for half in range(2):
            to_frame(k, half).wait_send()
        pairs_to(k).wait_send()
    if gathers:
        gather.close(0)
        gather.close(1)


def local(frames, count, frames_in, cotangent, w_qkv_space, w_out_space, w_qkv_time, w_out_time, neighbours):
    gathers = frames == 2 and count == 8 and w_qkv_space.shape[0] == 96
    blocks = [w_qkv_space, w_out_space, w_qkv_time, w_out_time]
    if not gathers:
        blocks = [lax.all_gather(block, "space", axis=0, tiled=True) for block in blocks]
    vmem = pl.BlockSpec(memory_space=pltpu.VMEM)
    hbm = pl.BlockSpec(memory_space=pl.ANY)
    dma = pltpu.SemaphoreType.DMA
    wide = (ROWS, 2 * D)
    out, grad = pl.pallas_call(
        functools.partial(kernel, frames, count, gathers),
        out_shape=[jax.ShapeDtypeStruct((ROWS, D), BF16)] * 2,
        in_specs=[vmem, vmem, hbm, hbm, hbm, hbm, pl.BlockSpec(memory_space=pltpu.SMEM)],
        out_specs=[vmem, vmem],
        scratch_shapes=[
            pltpu.VMEM((2, D, 4 * D), BF16),
            pltpu.VMEM((3 * ROWS, D), BF16),
            pltpu.VMEM((3 * ROWS, D), BF16),
            pltpu.VMEM((3 * ROWS, 3 * D), BF16),
            pltpu.VMEM((ROWS, D), BF16),
            pltpu.VMEM((PAIRS, 2 * ROWS, 3 * ROWS), F32),
            pltpu.VMEM((PAIRS, 4 * ROWS, ROWS), F32),
            pltpu.VMEM((ROWS, D), BF16),
            pltpu.VMEM((ROWS, D), BF16),
            pltpu.VMEM((2,) + wide, BF16),
            pltpu.VMEM((frames,) + wide, BF16),
            pltpu.VMEM((frames - 1, ROWS, 256), BF16),
            pltpu.VMEM((frames, ROWS, 256), BF16),
            pltpu.VMEM((ROWS, D), BF16),
            pltpu.VMEM((ROWS, 3 * D), BF16),
            pltpu.VMEM(wide, F32),
            pltpu.VMEM((3 * ROWS, D), BF16),
            pltpu.VMEM((ROWS, 128), F32),
            pltpu.VMEM((2, ROWS, 128), F32),
            pltpu.VMEM((ROWS, 128), F32),
            pltpu.VMEM((2, ROWS, 128), F32),
            pltpu.VMEM((ROWS, D), F32),
            dma((4,)),
            dma((2, 2, 4)), dma((2, 4)), dma((2, 4)), dma((2, 4)),
            dma((2, 8)), dma((2, 8)), dma((2, 8)), dma((2, 8)),
            *[dma((2,))] * 8,
            dma((frames - 1, 2)), dma((frames, 2)), dma((frames - 1,)), dma((frames,)),
        ],
        compiler_params=pltpu.CompilerParams(
            collective_id=0, has_side_effects=True, vmem_limit_bytes=56 * 1024 * 1024
        ),
    )(frames_in[0], cotangent[0], *blocks, neighbours)
    return out[None], grad[None]


def solution(mesh):
    rows = P(("dp", "frame"), "space", None)
    held = P("space", None)
    return jax.shard_map(
        functools.partial(local, mesh.shape["frame"], mesh.shape["space"]),
        mesh=mesh,
        in_specs=(rows, rows, held, held, held, held, P()),
        out_specs=(rows, rows),
        check_vma=False,
    )
```

```python
import functools

import jax
import jax.numpy as jnp
from jax import lax
from jax.experimental import pallas as pl
from jax.experimental.pallas import tpu as pltpu
from jax.sharding import PartitionSpec as P

HEADS = 12
HD = 64
D = 768
ROWS = 128
PAIRS = HEADS // 2
EPS = 1e-06
FAR = -1e30
SCALE = HD ** (-0.5)
F32 = jnp.float32
BF16 = jnp.bfloat16
TILE = 256


def dot(a, b):
    return jnp.dot(a, b, preferred_element_type=F32)


def dot_nt(a, b):
    return lax.dot_general(a, b, (((1,), (1,)), ((), ())), preferred_element_type=F32)


def dot_tn(a, b):
    return lax.dot_general(a, b, (((0,), (0,)), ((), ())), preferred_element_type=F32)


def rms_factor(values):
    return lax.rsqrt(jnp.mean(values * values, axis=-1, keepdims=True) + EPS)


def rms_back(values, upstream):
    factor = rms_factor(values)
    inner = jnp.mean(values * upstream, axis=-1, keepdims=True)
    return factor * upstream - values * (factor * factor * factor * inner)


def remote(src, dst, send, recv, where):
    return pltpu.make_async_remote_copy(
        src_ref=src,
        dst_ref=dst,
        send_sem=send,
        recv_sem=recv,
        device_id=where,
        device_id_type=pl.DeviceIdType.MESH,
    )


class Gather:
    X = 2
    Z = 4

    def __init__(self, weights, sems):
        self.w = weights
        self.zs, self.zr, self.xs, self.xr, self.ys, self.yr, self.cs, self.cr = sems
        self.s = lax.axis_index("space")
        self.z = self.s // self.X
        self.x = self.s % self.X
        self.odd = lax.axis_index("frame")
        self.c = lax.axis_index("dp")

    def rows(self, group, shard, offset, count):
        start = pl.multiple_of(shard * 96 + offset, 16)
        return self.w.at[group, pl.ds(start, count), :]

    def main(self, group, shard):
        return self.rows(group, shard, 48 * self.c + 16 * self.odd, 32)

    def along_z(self, group, step, at):
        ref = self.main(group, at * self.X + self.x)
        way = 0 if step > 0 else 1
        return remote(
            ref, ref, self.zs.at[group, way, at], self.zr.at[group, at], {"space": self.s + step * self.X}
        )

    def along_x(self, group, at, column):
        ref = self.main(group, at * self.X + column)
        partner = self.s + 1 - 2 * self.x
        return remote(ref, ref, self.xs.at[group, at], self.xr.at[group, at], {"space": partner})

    def along_y(self, group, shard, sending):
        which = self.odd if sending else 1 - self.odd
        ref = self.rows(group, shard, 48 * self.c + 32 * which, 16)
        return remote(
            ref, ref, self.ys.at[group, shard], self.yr.at[group, shard], {"frame": 1 - self.odd}
        )

    def across(self, group, shard, sending):
        half = self.c if sending else 1 - self.c
        ref = self.rows(group, shard, 48 * half, 48)
        return remote(
            ref, ref, self.cs.at[group, shard], self.cr.at[group, shard], {"dp": 1 - self.c}
        )

    def open(self, group):
        @pl.when(self.z < self.Z - 1)
        def _():
            self.along_z(group, 1, self.z).start()

        @pl.when(self.z > 0)
        def _():
            self.along_z(group, -1, self.z).start()

        self.along_x(group, self.z, self.x).start()

    def z_step(self, group, distance):
        for step in (1, -1):
            at = self.z - step * distance

            @pl.when((at >= 0) & (at < self.Z))
            def _():
                self.along_z(group, -step, at).wait_recv()
                onward = (self.z + step >= 0) & (self.z + step < self.Z)

                @pl.when(onward)
                def _():
                    self.along_z(group, step, at).start()

                self.along_x(group, at, self.x).start()
                self.along_y(group, at * self.X + self.x, True).start()

    def x_step(self, group, distance):
        for step in (1, -1) if distance else (1,):
            at = self.z - step * distance

            @pl.when((at >= 0) & (at < self.Z))
            def _():
                self.along_x(group, at, 1 - self.x).wait_recv()
                self.along_y(group, at * self.X + 1 - self.x, True).start()

    def others(self):
        count = self.X * self.Z
        return [lax.rem(self.s + k, count) for k in range(1, count)]

    def y_stage(self, group):
        for shard in self.others():
            self.along_y(group, shard, False).wait_recv()
            self.across(group, shard, True).start()

    def c_stage(self, group):
        for shard in self.others():
            self.across(group, shard, False).wait_recv()

    def close(self, group):
        for at in range(self.Z):

            @pl.when((self.z < self.Z - 1) & (at <= self.z))
            def _():
                self.along_z(group, 1, at).wait_send()

            @pl.when((self.z > 0) & (at >= self.z))
            def _():
                self.along_z(group, -1, at).wait_send()

            self.along_x(group, at, self.x).wait_send()
        for shard in self.others():
            self.along_y(group, shard, True).wait_send()
            self.across(group, shard, True).wait_send()


def kernel(
    frames, count, gathers,
    x_ref, cot_ref, wqs_ref, wos_ref, wqt_ref, wot_ref, nb_ref,
    out_ref, grad_ref,
    weights, x_win, normed, qkv, att, probs, near_probs, streams, cots, normed_t, qkv_t, ga_t, shares_t, score_t,
    rows_a, attn_t, grads, gown, ga_win, tot, tot_got, dlt, dlt_got, acc,
    load_sem, zs, zr, xs, xr, ys, yr, cs, cr, hs, hr, bs, br, ds, dr, es, er, ts, tr, us, ur,
):
    s = lax.axis_index("space")
    f = lax.axis_index("frame")
    c = lax.axis_index("dp")

    barrier = pltpu.get_barrier_semaphore()
    peers = [{"space": lax.rem(s + k, count)} for k in (1, 2, count - 2, count - 1)]
    peers += [{"frame": lax.rem(f + k, frames)} for k in range(1, frames)]
    peers += [{"dp": 1 - c}]
    for peer in peers:
        pl.semaphore_signal(barrier, inc=1, device_id=peer, device_id_type=pl.DeviceIdType.MESH)

    depth = wqs_ref.shape[0]
    start = pl.multiple_of(s * depth, 16) if gathers else 0
    here = pl.ds(start, depth)
    loads = [
        pltpu.make_async_copy(ref, weights.at[group, here, pl.ds(col, ref.shape[1])], load_sem.at[i])
        for i, (ref, group, col) in enumerate(
            ((wqs_ref, 0, 0), (wos_ref, 0, 3 * D), (wqt_ref, 1, 0), (wot_ref, 1, 3 * D))
        )
    ]
    for load in loads:
        load.start()

    lane = lax.broadcasted_iota(jnp.int32, (1, 2 * HD), 1)
    first = lane < HD
    first_row = first.astype(F32).astype(BF16)
    second_row = (1.0 - first.astype(F32)).astype(BF16)

    def stacked(pair):
        return jnp.concatenate([pair * first_row, pair * second_row], axis=0)

    def joined(both):
        return jnp.where(first, both[:ROWS], both[ROWS:])

    def forward(rows, group, col, width, put):
        for at in range(0, width, TILE):
            put(at, dot(rows[...], weights[group, :, pl.ds(col + at, TILE)]))

    def backward(rows, cols, group, put):
        for at in range(0, D, TILE):
            put(at, dot_nt(rows[...], weights[group, pl.ds(at, TILE), cols]))

    def into(ref, col=0):
        def put(at, value):
            ref[:, pl.ds(col + at, TILE)] = value.astype(ref.dtype)

        return put

    own = pl.ds(ROWS, ROWS)
    sides = (pl.ds(0, ROWS), pl.ds(2 * ROWS, ROWS))
    has = [s > 0, s < count - 1]

    def two_ways(src, slots, send, recv):
        return [
            remote(src, slots[1 - way], send.at[way], recv.at[way], {"space": s + 2 * way - 1})
            for way in range(2)
        ]

    def each_way(action):
        for way in range(2):
            pl.when(has[way])(functools.partial(action, way))

    def leave(copies):
        each_way(lambda way: copies[way].start())

    def arrive(copies):
        each_way(lambda way: copies[1 - way].wait_recv())

    x_halo = two_ways(x_ref, [x_win.at[side, :] for side in sides], hs, hr)
    ga_halo = two_ways(ga_win.at[own, :], [ga_win.at[side, :] for side in sides], bs, br)
    tot_halo = two_ways(tot, [tot_got.at[way] for way in range(2)], ds, dr)
    dlt_halo = two_ways(dlt, [dlt_got.at[way] for way in range(2)], es, er)

    mine = pl.ds(pl.multiple_of(f * ROWS, ROWS), ROWS)

    def frame_copies(src, held, send, recv):
        out, got = [], []
        for k in range(1, frames):
            o = lax.rem(f + k, frames)
            theirs = pl.ds(pl.multiple_of(o * ROWS, ROWS), ROWS)
            where = {"frame": o}
            out.append(remote(src, held.at[mine, :], send.at[k - 1], recv.at[f], where))
            got.append(remote(src, held.at[theirs, :], send.at[k - 1], recv.at[o], where))
        return out, got

    cot_out, cot_got = frame_copies(cot_ref, cots, ts, tr)
    stream_out, stream_got = frame_copies(streams.at[mine, :], streams, us, ur)
    cots[mine, :] = cot_ref[...]
    x_win[own, :] = x_ref[...]
    for way in range(2):

        @pl.when(jnp.logical_not(has[way]))
        def _():
            x_win[sides[way], :] = jnp.zeros((ROWS, D), BF16)
            ga_win[sides[way], :] = jnp.zeros((ROWS, D), BF16)
            tot_got[way] = jnp.ones((16, 128), F32)
            dlt_got[way] = jnp.zeros((16, 128), F32)

    pl.semaphore_wait(barrier, len(peers))
    leave(x_halo)
    for copy in cot_out:
        copy.start()
    for load in loads:
        load.wait()
    gather = Gather(weights, (zs, zr, xs, xr, ys, yr, cs, cr)) if gathers else None

    def pass_on(*steps):
        if gathers:
            for name, *where in steps:
                getattr(gather, name)(*where)

    pass_on(
        ("open", 0),
        ("z_step", 0, 1), ("x_step", 0, 0), ("z_step", 0, 2), ("open", 1), ("x_step", 0, 1), ("z_step", 0, 3),
        ("x_step", 0, 2), ("z_step", 1, 1), ("x_step", 0, 3),
    )
    arrive(x_halo)
    values = x_win[...].astype(F32)
    normed[...] = (values * rms_factor(values)).astype(BF16)
    pass_on(("y_stage", 0), ("z_step", 1, 2), ("x_step", 1, 0), ("c_stage", 0))
    forward(normed, 0, 0, D, into(qkv))
    pass_on(("z_step", 1, 3), ("x_step", 1, 1))
    forward(normed, 0, D, 2 * D, into(qkv, D))
    pass_on(("x_step", 1, 2), ("x_step", 1, 3))

    def listed(block):
        hit = nb_ref[s, 0] == block
        for j in range(1, nb_ref.shape[1]):
            hit = hit | (nb_ref[s, j] == block)
        return jnp.where(hit, 0.0, FAR).astype(F32)

    key_lane = lax.broadcasted_iota(jnp.int32, (1, 3 * ROWS), 1)
    bias = jnp.where(
        key_lane < ROWS, listed(s - 1), jnp.where(key_lane < 2 * ROWS, listed(s), listed(s + 1))
    )

    head_lane = lax.broadcasted_iota(jnp.int32, (1, 128), 1)

    def cols_of(hp, part):
        return pl.ds(part * D + hp * 128, 128)

    def attend(hp, totals):
        cols = cols_of(hp, 0)
        scores = dot_nt(stacked(qkv[own, cols]), qkv[:, cols_of(hp, 1)]) * SCALE + bias
        expo = jnp.exp(scores)
        total = jnp.sum(expo, axis=-1, keepdims=True)
        weight = expo / total
        probs[hp] = weight
        att[:, cols] = joined(dot(weight.astype(BF16), qkv[:, cols_of(hp, 2)])).astype(BF16)
        totals = jnp.where(head_lane == 2 * hp, total[:ROWS], totals)
        return jnp.where(head_lane == 2 * hp + 1, total[ROWS:], totals)

    totals = jnp.ones((ROWS, 128), F32)
    for hp in range(PAIRS):
        totals = attend(hp, totals)
    tot[...] = totals.T[:16]
    leave(tot_halo)

    forward(att, 0, 3 * D, D, into(acc))
    streams[mine, :] = (x_ref[...].astype(F32) + acc[...]).astype(BF16)
    for copy in stream_out:
        copy.start()
    pass_on(("y_stage", 1))

    def listed_by(block):
        row = jnp.clip(block, 0, count - 1)
        hit = nb_ref[row, 0] == s
        for j in range(1, nb_ref.shape[1]):
            hit = hit | (nb_ref[row, j] == s)
        return jnp.where(hit & (block >= 0) & (block < count), 0.0, FAR).astype(F32)

    def both_sides(window, cols):
        return jnp.concatenate([stacked(window[side, cols]) for side in sides], axis=0)

    def column(held, hp):
        return [
            jnp.sum(jnp.where(head_lane == 2 * hp + i, held, 0.0), axis=-1, keepdims=True)
            for i in range(2)
        ]

    def near_lanes(held, hp):
        return jnp.concatenate(
            [held[way, 2 * hp + i : 2 * hp + i + 1, :] for way in range(2) for i in range(2)], axis=1
        )

    near_row = lax.broadcasted_iota(jnp.int32, (1, 4 * ROWS), 1)
    near_bias = jnp.where(near_row < 2 * ROWS, listed_by(s - 1), listed_by(s + 1))

    def near(hp):
        query_four = both_sides(qkv, cols_of(hp, 0))
        scores = dot_nt(qkv[own, cols_of(hp, 1)], query_four) * SCALE + near_bias
        near_probs[hp] = jnp.exp(scores) / near_lanes(tot_got, hp)

    arrive(tot_halo)
    for hp in range(PAIRS):
        near(hp)

    pass_on(("c_stage", 1))
    for copy in stream_got + cot_got:
        copy.wait_recv()
    values = streams[...].astype(F32)
    normed_t[...] = (values * rms_factor(values)).astype(BF16)
    forward(normed_t, 1, 0, 3 * D, into(qkv_t))
    backward(cots, pl.ds(3 * D, D), 1, into(ga_t))

    hot = (
        lax.broadcasted_iota(jnp.int32, (D, 128), 0) // HD
        == lax.broadcasted_iota(jnp.int32, (D, 128), 1)
    ).astype(F32).astype(BF16)

    def per_head(product):
        high = product.astype(BF16)
        low = (product - high.astype(F32)).astype(BF16)
        return dot(high, hot) + dot(low, hot)

    def spread(heads):
        return dot_nt(heads, hot)

    def frame_rows(i):
        return pl.ds(i * ROWS, ROWS)

    def part(i, which):
        return qkv_t[frame_rows(i), which * D : (which + 1) * D].astype(F32)

    for i in range(frames):
        query = part(i, 0)
        grad_att = ga_t[frame_rows(i), :].astype(F32)
        expos = [jnp.exp(per_head(query * part(g, 1)) * SCALE) for g in range(i + 1)]
        prob_grads = [per_head(grad_att * part(g, 2)) for g in range(i + 1)]
        total = sum(expos[1:], expos[0])
        shares = [expo / total for expo in expos]
        rounded = [share.astype(BF16) for share in shares]
        terms = [prob.astype(F32) * grad for prob, grad in zip(rounded, prob_grads)]
        delta = sum(terms[1:], terms[0])
        for g in range(frames):
            if g <= i:
                shares_t[i, g] = rounded[g]
                score_t[i, g] = (shares[g] * (prob_grads[g] - delta)).astype(BF16)
            else:
                shares_t[i, g] = jnp.zeros((ROWS, 128), BF16)
                score_t[i, g] = jnp.zeros((ROWS, 128), BF16)

    def over_frames(term):
        total = term(0)
        for i in range(1, frames):
            total = total + term(i)
        return total

    attn_t[...] = over_frames(lambda g: spread(shares_t[f, g]) * part(g, 2)).astype(BF16)
    grads[:, 0:D] = (over_frames(lambda g: spread(score_t[f, g]) * part(g, 1)) * SCALE).astype(BF16)
    grads[:, D : 2 * D] = (
        over_frames(lambda i: spread(score_t[i, f]) * part(i, 0)) * SCALE
    ).astype(BF16)
    grads[:, 2 * D : 3 * D] = over_frames(
        lambda i: spread(shares_t[i, f]) * ga_t[frame_rows(i), :].astype(F32)
    ).astype(BF16)

    def put_out(at, value):
        cols = pl.ds(at, TILE)
        out_ref[:, cols] = (streams[mine, cols].astype(F32) + value).astype(BF16)

    backward(grads, pl.ds(0, 3 * D), 1, into(acc))
    rows_a[...] = (
        cot_ref[...].astype(F32) + rms_back(streams[mine, :].astype(F32), acc[...])
    ).astype(BF16)

    def put_ga(at, value):
        ga_win[own, pl.ds(at, TILE)] = value.astype(BF16)

    backward(rows_a, pl.ds(3 * D, D), 0, put_ga)
    leave(ga_halo)
    deltas = per_head(ga_win[own, :].astype(F32) * att[...].astype(F32))
    dlt[...] = deltas.T[:16]
    leave(dlt_halo)

    def attend_back(hp):
        cols = cols_of(hp, 0)
        grad_two = stacked(ga_win[own, cols])
        weight = probs[hp]
        grad_prob = dot_nt(grad_two, qkv[:, cols_of(hp, 2)])
        row_delta = jnp.concatenate(column(deltas, hp), axis=0)
        score_grad = (weight * (grad_prob - row_delta)).astype(BF16)
        grads[:, cols] = (joined(dot(score_grad, qkv[:, cols_of(hp, 1)])) * SCALE).astype(BF16)
        middle = slice(ROWS, 2 * ROWS)
        gown[:, cols] = dot_tn(score_grad[:, middle], stacked(qkv[own, cols]))
        gown[:, cols_of(hp, 1)] = dot_tn(weight[:, middle].astype(BF16), grad_two)

    for hp in range(PAIRS):
        attend_back(hp)
    forward(attn_t, 1, 3 * D, D, put_out)
    backward(grads.at[:, pl.ds(0, D)], pl.ds(0, D), 0, into(acc))
    arrive(ga_halo)
    arrive(dlt_halo)

    def near_back(hp):
        cols = cols_of(hp, 0)
        grad_four = both_sides(ga_win, cols)
        weight = near_probs[hp]
        grad_prob = dot_nt(qkv[own, cols_of(hp, 2)], grad_four)
        score_grad = (weight * (grad_prob - near_lanes(dlt_got, hp))).astype(BF16)
        key_grad = gown[:, cols] + dot(score_grad, both_sides(qkv, cols))
        value_grad = gown[:, cols_of(hp, 1)] + dot(weight.astype(BF16), grad_four)
        grads[:, cols_of(hp, 1)] = (key_grad * SCALE).astype(BF16)
        grads[:, cols_of(hp, 2)] = value_grad.astype(BF16)

    for hp in range(PAIRS):
        near_back(hp)

    def put_more(at, value):
        cols = pl.ds(at, TILE)
        acc[:, cols] = acc[:, cols] + value

    backward(grads.at[:, pl.ds(D, 2 * D)], pl.ds(D, 2 * D), 0, put_more)
    grad_ref[...] = (
        rows_a[...].astype(F32) + rms_back(x_ref[...].astype(F32), acc[...])
    ).astype(BF16)

    for copies in (x_halo, tot_halo, ga_halo, dlt_halo):
        each_way(lambda way: copies[way].wait_send())
    for copy in cot_out + stream_out:
        copy.wait_send()
    if gathers:
        gather.close(0)
        gather.close(1)


def local(frames, count, frames_in, cotangent, w_qkv_space, w_out_space, w_qkv_time, w_out_time, neighbours):
    gathers = frames == 2 and count == 8 and w_qkv_space.shape[0] == 96
    blocks = [w_qkv_space, w_out_space, w_qkv_time, w_out_time]
    if not gathers:
        blocks = [lax.all_gather(block, "space", axis=0, tiled=True) for block in blocks]
    vmem = pl.BlockSpec(memory_space=pltpu.VMEM)
    hbm = pl.BlockSpec(memory_space=pl.ANY)
    dma = pltpu.SemaphoreType.DMA
    wide = (ROWS, 2 * D)
    out, grad = pl.pallas_call(
        functools.partial(kernel, frames, count, gathers),
        out_shape=[jax.ShapeDtypeStruct((ROWS, D), BF16)] * 2,
        in_specs=[vmem, vmem, hbm, hbm, hbm, hbm, pl.BlockSpec(memory_space=pltpu.SMEM)],
        out_specs=[vmem, vmem],
        scratch_shapes=[
            pltpu.VMEM((2, D, 4 * D), BF16),
            pltpu.VMEM((3 * ROWS, D), BF16),
            pltpu.VMEM((3 * ROWS, D), BF16),
            pltpu.VMEM((3 * ROWS, 3 * D), BF16),
            pltpu.VMEM((ROWS, D), BF16),
            pltpu.VMEM((PAIRS, 2 * ROWS, 3 * ROWS), F32),
            pltpu.VMEM((PAIRS, ROWS, 4 * ROWS), F32),
            *[pltpu.VMEM((frames * ROWS, D), BF16)] * 3,
            pltpu.VMEM((frames * ROWS, 3 * D), BF16),
            pltpu.VMEM((frames * ROWS, D), BF16),
            *[pltpu.VMEM((frames, frames, ROWS, 128), BF16)] * 2,
            pltpu.VMEM((ROWS, D), BF16),
            pltpu.VMEM((ROWS, D), BF16),
            pltpu.VMEM((ROWS, 3 * D), BF16),
            pltpu.VMEM(wide, F32),
            pltpu.VMEM((3 * ROWS, D), BF16),
            *[pltpu.VMEM((16, 128), F32), pltpu.VMEM((2, 16, 128), F32)] * 2,
            pltpu.VMEM((ROWS, D), F32),
            dma((4,)),
            dma((2, 2, 4)), dma((2, 4)), dma((2, 4)), dma((2, 4)),
            dma((2, 8)), dma((2, 8)), dma((2, 8)), dma((2, 8)),
            *[dma((2,))] * 8,
            *[dma((frames - 1,)), dma((frames,))] * 2,
        ],
        compiler_params=pltpu.CompilerParams(
            collective_id=0, has_side_effects=True, vmem_limit_bytes=56 * 1024 * 1024
        ),
    )(frames_in[0], cotangent[0], *blocks, neighbours)
    return out[None], grad[None]


def solution(mesh):
    rows = P(("dp", "frame"), "space", None)
    held = P("space", None)
    return jax.shard_map(
        functools.partial(local, mesh.shape["frame"], mesh.shape["space"]),
        mesh=mesh,
        in_specs=(rows, rows, held, held, held, held, P()),
        out_specs=(rows, rows),
        check_vma=False,
    )
```

```python
import functools

import jax
import jax.numpy as jnp
from jax import lax
from jax.experimental import pallas as pl
from jax.experimental.pallas import tpu as pltpu
from jax.sharding import PartitionSpec as P

HEADS = 12
HD = 64
D = 768
ROWS = 128
PAIRS = HEADS // 2
EPS = 1e-06
FAR = -1e30
SCALE = HD ** (-0.5)
F32 = jnp.float32
BF16 = jnp.bfloat16
TILE = 256


def dot(a, b):
    return jnp.dot(a, b, preferred_element_type=F32)


def dot_nt(a, b):
    return lax.dot_general(a, b, (((1,), (1,)), ((), ())), preferred_element_type=F32)


def dot_tn(a, b):
    return lax.dot_general(a, b, (((0,), (0,)), ((), ())), preferred_element_type=F32)


def rms_factor(values):
    return lax.rsqrt(jnp.mean(values * values, axis=-1, keepdims=True) + EPS)


def rms_back(values, upstream):
    factor = rms_factor(values)
    inner = jnp.mean(values * upstream, axis=-1, keepdims=True)
    return factor * upstream - values * (factor * factor * factor * inner)


def remote(src, dst, send, recv, where):
    return pltpu.make_async_remote_copy(
        src_ref=src,
        dst_ref=dst,
        send_sem=send,
        recv_sem=recv,
        device_id=where,
        device_id_type=pl.DeviceIdType.MESH,
    )


class Gather:
    X = 2
    Z = 4

    def __init__(self, weights, sems):
        self.w = weights
        self.zs, self.zr, self.xs, self.xr, self.ys, self.yr, self.cs, self.cr, self.ps, self.pr = sems
        self.s = lax.axis_index("space")
        self.z = self.s // self.X
        self.x = self.s % self.X
        self.pair = self.z + 1 - 2 * (self.z % 2)
        self.odd = lax.axis_index("frame")
        self.c = lax.axis_index("dp")

    def rows(self, group, shard, offset, count):
        start = pl.multiple_of(shard * 96 + offset, 16)
        return self.w.at[group, pl.ds(start, count), :]

    def main(self, group, shard):
        return self.rows(group, shard, 48 * self.c + 16 * self.odd, 32)

    def along_z(self, group, step, at):
        ref = self.main(group, at * self.X + self.x)
        way = 0 if step > 0 else 1
        return remote(
            ref, ref, self.zs.at[group, way, at], self.zr.at[group, at], {"space": self.s + step * self.X}
        )

    def along_x(self, group, at, column):
        ref = self.main(group, at * self.X + column)
        partner = self.s + 1 - 2 * self.x
        return remote(ref, ref, self.xs.at[group, at], self.xr.at[group, at], {"space": partner})

    def to_pair(self, group, at):
        ref = self.main(group, at * self.X + 1 - self.x)
        where = {"space": self.s + (self.pair - self.z) * self.X}
        return remote(ref, ref, self.ps.at[group], self.pr.at[group], where)

    def along_y(self, group, shard, sending):
        which = self.odd if sending else 1 - self.odd
        ref = self.rows(group, shard, 48 * self.c + 32 * which, 16)
        return remote(
            ref, ref, self.ys.at[group, shard], self.yr.at[group, shard], {"frame": 1 - self.odd}
        )

    def across(self, group, shard, sending):
        half = self.c if sending else 1 - self.c
        ref = self.rows(group, shard, 48 * half, 48)
        return remote(
            ref, ref, self.cs.at[group, shard], self.cr.at[group, shard], {"dp": 1 - self.c}
        )

    def open(self, group):
        @pl.when(self.z < self.Z - 1)
        def _():
            self.along_z(group, 1, self.z).start()

        @pl.when(self.z > 0)
        def _():
            self.along_z(group, -1, self.z).start()

        self.along_x(group, self.z, self.x).start()

    def z_step(self, group, distance):
        for step in (1, -1):
            at = self.z - step * distance

            @pl.when((at >= 0) & (at < self.Z))
            def _():
                self.along_z(group, -step, at).wait_recv()
                onward = (self.z + step >= 0) & (self.z + step < self.Z)

                @pl.when(onward)
                def _():
                    self.along_z(group, step, at).start()

                pl.when(at != self.pair)(lambda: self.along_x(group, at, self.x).start())
                self.along_y(group, at * self.X + self.x, True).start()

    def x_step(self, group, distance):
        for step in (1, -1) if distance else (1,):
            at = self.z - step * distance

            @pl.when((at >= 0) & (at < self.Z))
            def _():
                pl.when(at != self.pair)(lambda: self.along_x(group, at, 1 - self.x).wait_recv())
                pl.when(at == self.pair)(lambda: self.to_pair(group, at).wait_recv())
                if distance == 0:
                    self.to_pair(group, at).start()
                self.along_y(group, at * self.X + 1 - self.x, True).start()

    def others(self):
        count = self.X * self.Z
        return [lax.rem(self.s + k, count) for k in range(1, count)]

    def y_stage(self, group):
        for shard in self.others():
            self.along_y(group, shard, False).wait_recv()
            self.across(group, shard, True).start()

    def c_stage(self, group):
        for shard in self.others():
            self.across(group, shard, False).wait_recv()

    def close(self, group):
        for at in range(self.Z):

            @pl.when((self.z < self.Z - 1) & (at <= self.z))
            def _():
                self.along_z(group, 1, at).wait_send()

            @pl.when((self.z > 0) & (at >= self.z))
            def _():
                self.along_z(group, -1, at).wait_send()

            pl.when(at != self.pair)(lambda: self.along_x(group, at, self.x).wait_send())
        self.to_pair(group, self.z).wait_send()
        for shard in self.others():
            self.along_y(group, shard, True).wait_send()
            self.across(group, shard, True).wait_send()


def kernel(
    frames, count, gathers,
    x_ref, cot_ref, wqs_ref, wos_ref, wqt_ref, wot_ref, nb_ref,
    out_ref, grad_ref,
    weights, x_win, normed, qkv, att, probs, near_probs, streams, cots, normed_t, qkv_t, ga_t, shares_t, score_t,
    rows_a, attn_t, grads, gown, ga_win, tot, tot_got, dlt, dlt_got, acc,
    load_sem, zs, zr, xs, xr, ys, yr, cs, cr, ps, pr, hs, hr, bs, br, ds, dr, es, er, ts, tr, us, ur,
):
    s = lax.axis_index("space")
    f = lax.axis_index("frame")
    c = lax.axis_index("dp")

    barrier = pltpu.get_barrier_semaphore()
    peers = [{"space": lax.rem(s + k, count)} for k in (1, 2, count - 2, count - 1)]
    peers += [{"frame": lax.rem(f + k, frames)} for k in range(1, frames)]
    peers += [{"dp": 1 - c}]
    for peer in peers:
        pl.semaphore_signal(barrier, inc=1, device_id=peer, device_id_type=pl.DeviceIdType.MESH)

    depth = wqs_ref.shape[0]
    start = pl.multiple_of(s * depth, 16) if gathers else 0
    here = pl.ds(start, depth)
    loads = [
        pltpu.make_async_copy(ref, weights.at[group, here, pl.ds(col, ref.shape[1])], load_sem.at[i])
        for i, (ref, group, col) in enumerate(
            ((wqs_ref, 0, 0), (wos_ref, 0, 3 * D), (wqt_ref, 1, 0), (wot_ref, 1, 3 * D))
        )
    ]
    for load in loads:
        load.start()

    lane = lax.broadcasted_iota(jnp.int32, (1, 2 * HD), 1)
    first = lane < HD
    first_row = first.astype(F32).astype(BF16)
    second_row = (1.0 - first.astype(F32)).astype(BF16)

    def stacked(pair):
        return jnp.concatenate([pair * first_row, pair * second_row], axis=0)

    def joined(both):
        return jnp.where(first, both[:ROWS], both[ROWS:])

    def forward(rows, group, col, width, put):
        for at in range(0, width, TILE):
            put(at, dot(rows[...], weights[group, :, pl.ds(col + at, TILE)]))

    def backward(rows, cols, group, put):
        for at in range(0, D, TILE):
            put(at, dot_nt(rows[...], weights[group, pl.ds(at, TILE), cols]))

    def into(ref, col=0):
        def put(at, value):
            ref[:, pl.ds(col + at, TILE)] = value.astype(ref.dtype)

        return put

    own = pl.ds(ROWS, ROWS)
    sides = (pl.ds(0, ROWS), pl.ds(2 * ROWS, ROWS))
    has = [s > 0, s < count - 1]

    def two_ways(src, slots, send, recv):
        return [
            remote(src, slots[1 - way], send.at[way], recv.at[way], {"space": s + 2 * way - 1})
            for way in range(2)
        ]

    def each_way(action):
        for way in range(2):
            pl.when(has[way])(functools.partial(action, way))

    def leave(copies):
        each_way(lambda way: copies[way].start())

    def arrive(copies):
        each_way(lambda way: copies[1 - way].wait_recv())

    x_halo = two_ways(x_ref, [x_win.at[side, :] for side in sides], hs, hr)
    thirds = [pl.ds(at, TILE) for at in range(0, D, TILE)]
    ga_halo = [
        two_ways(
            ga_win.at[own, cols], [ga_win.at[side, cols] for side in sides], bs.at[i], br.at[i]
        )
        for i, cols in enumerate(thirds)
    ]
    tot_halo = two_ways(tot, [tot_got.at[way] for way in range(2)], ds, dr)
    dlt_halo = two_ways(dlt, [dlt_got.at[way] for way in range(2)], es, er)

    mine = pl.ds(pl.multiple_of(f * ROWS, ROWS), ROWS)

    def frame_copies(src, held, send, recv):
        out, got = [], []
        for k in range(1, frames):
            o = lax.rem(f + k, frames)
            theirs = pl.ds(pl.multiple_of(o * ROWS, ROWS), ROWS)
            where = {"frame": o}
            out.append(remote(src, held.at[mine, :], send.at[k - 1], recv.at[f], where))
            got.append(remote(src, held.at[theirs, :], send.at[k - 1], recv.at[o], where))
        return out, got

    cot_out, cot_got = frame_copies(cot_ref, cots, ts, tr)
    stream_out, stream_got = frame_copies(streams.at[mine, :], streams, us, ur)
    cots[mine, :] = cot_ref[...]
    x_win[own, :] = x_ref[...]
    for way in range(2):

        @pl.when(jnp.logical_not(has[way]))
        def _():
            x_win[sides[way], :] = jnp.zeros((ROWS, D), BF16)
            ga_win[sides[way], :] = jnp.zeros((ROWS, D), BF16)
            tot_got[way] = jnp.ones((16, 128), F32)
            dlt_got[way] = jnp.zeros((16, 128), F32)

    pl.semaphore_wait(barrier, len(peers))
    leave(x_halo)
    for copy in cot_out:
        copy.start()
    for load in loads:
        load.wait()
    gather = Gather(weights, (zs, zr, xs, xr, ys, yr, cs, cr, ps, pr)) if gathers else None

    def pass_on(*steps):
        if gathers:
            for name, *where in steps:
                getattr(gather, name)(*where)

    pass_on(
        ("open", 0),
        ("z_step", 0, 1), ("x_step", 0, 0), ("z_step", 0, 2), ("open", 1), ("x_step", 0, 1), ("z_step", 0, 3),
        ("x_step", 0, 2), ("z_step", 1, 1), ("x_step", 0, 3),
    )
    arrive(x_halo)
    values = x_win[...].astype(F32)
    normed[...] = (values * rms_factor(values)).astype(BF16)
    pass_on(("y_stage", 0), ("z_step", 1, 2), ("x_step", 1, 0), ("c_stage", 0))
    forward(normed, 0, 0, D, into(qkv))
    pass_on(("z_step", 1, 3), ("x_step", 1, 1))
    forward(normed, 0, D, 2 * D, into(qkv, D))
    pass_on(("x_step", 1, 2), ("x_step", 1, 3))

    def listed(block):
        hit = nb_ref[s, 0] == block
        for j in range(1, nb_ref.shape[1]):
            hit = hit | (nb_ref[s, j] == block)
        return jnp.where(hit, 0.0, FAR).astype(F32)

    key_lane = lax.broadcasted_iota(jnp.int32, (1, 3 * ROWS), 1)
    bias = jnp.where(
        key_lane < ROWS, listed(s - 1), jnp.where(key_lane < 2 * ROWS, listed(s), listed(s + 1))
    )

    head_lane = lax.broadcasted_iota(jnp.int32, (1, 128), 1)

    def cols_of(hp, part):
        return pl.ds(part * D + hp * 128, 128)

    def attend(hp, totals):
        cols = cols_of(hp, 0)
        scores = dot_nt(stacked(qkv[own, cols]), qkv[:, cols_of(hp, 1)]) * SCALE + bias
        expo = jnp.exp(scores)
        total = jnp.sum(expo, axis=-1, keepdims=True)
        weight = expo / total
        probs[hp] = weight
        att[:, cols] = joined(dot(weight.astype(BF16), qkv[:, cols_of(hp, 2)])).astype(BF16)
        totals = jnp.where(head_lane == 2 * hp, total[:ROWS], totals)
        return jnp.where(head_lane == 2 * hp + 1, total[ROWS:], totals)

    totals = jnp.ones((ROWS, 128), F32)
    for hp in range(PAIRS):
        totals = attend(hp, totals)
    tot[...] = totals.T[:16]
    leave(tot_halo)

    forward(att, 0, 3 * D, D, into(acc))
    streams[mine, :] = (x_ref[...].astype(F32) + acc[...]).astype(BF16)
    for copy in stream_out:
        copy.start()
    pass_on(("y_stage", 1))

    def listed_by(block):
        row = jnp.clip(block, 0, count - 1)
        hit = nb_ref[row, 0] == s
        for j in range(1, nb_ref.shape[1]):
            hit = hit | (nb_ref[row, j] == s)
        return jnp.where(hit & (block >= 0) & (block < count), 0.0, FAR).astype(F32)

    def both_sides(window, cols):
        return jnp.concatenate([stacked(window[side, cols]) for side in sides], axis=0)

    def column(held, hp):
        return [
            jnp.sum(jnp.where(head_lane == 2 * hp + i, held, 0.0), axis=-1, keepdims=True)
            for i in range(2)
        ]

    def near_lanes(held, hp):
        return jnp.concatenate(
            [held[way, 2 * hp + i : 2 * hp + i + 1, :] for way in range(2) for i in range(2)], axis=1
        )

    near_row = lax.broadcasted_iota(jnp.int32, (1, 4 * ROWS), 1)
    near_bias = jnp.where(near_row < 2 * ROWS, listed_by(s - 1), listed_by(s + 1))

    def near(hp):
        query_four = both_sides(qkv, cols_of(hp, 0))
        scores = dot_nt(qkv[own, cols_of(hp, 1)], query_four) * SCALE + near_bias
        near_probs[hp] = jnp.exp(scores) / near_lanes(tot_got, hp)

    arrive(tot_halo)
    for hp in range(PAIRS):
        near(hp)

    pass_on(("c_stage", 1))
    for copy in stream_got + cot_got:
        copy.wait_recv()
    values = streams[...].astype(F32)
    normed_t[...] = (values * rms_factor(values)).astype(BF16)
    forward(normed_t, 1, 0, 3 * D, into(qkv_t))
    backward(cots, pl.ds(3 * D, D), 1, into(ga_t))

    hot = (
        lax.broadcasted_iota(jnp.int32, (D, 128), 0) // HD
        == lax.broadcasted_iota(jnp.int32, (D, 128), 1)
    ).astype(F32).astype(BF16)

    def per_head(product):
        high = product.astype(BF16)
        low = (product - high.astype(F32)).astype(BF16)
        return dot(high, hot) + dot(low, hot)

    def spread(heads):
        return dot_nt(heads, hot)

    def frame_rows(i):
        return pl.ds(i * ROWS, ROWS)

    def part(i, which):
        return qkv_t[frame_rows(i), which * D : (which + 1) * D].astype(F32)

    for i in range(frames):
        query = part(i, 0)
        grad_att = ga_t[frame_rows(i), :].astype(F32)
        expos = [jnp.exp(per_head(query * part(g, 1)) * SCALE) for g in range(i + 1)]
        prob_grads = [per_head(grad_att * part(g, 2)) for g in range(i + 1)]
        total = sum(expos[1:], expos[0])
        shares = [expo / total for expo in expos]
        rounded = [share.astype(BF16) for share in shares]
        terms = [prob.astype(F32) * grad for prob, grad in zip(rounded, prob_grads)]
        delta = sum(terms[1:], terms[0])
        for g in range(frames):
            if g <= i:
                shares_t[i, g] = rounded[g]
                score_t[i, g] = (shares[g] * (prob_grads[g] - delta)).astype(BF16)
            else:
                shares_t[i, g] = jnp.zeros((ROWS, 128), BF16)
                score_t[i, g] = jnp.zeros((ROWS, 128), BF16)

    def over_frames(term):
        total = term(0)
        for i in range(1, frames):
            total = total + term(i)
        return total

    attn_t[...] = over_frames(lambda g: spread(shares_t[f, g]) * part(g, 2)).astype(BF16)
    grads[:, 0:D] = (over_frames(lambda g: spread(score_t[f, g]) * part(g, 1)) * SCALE).astype(BF16)
    grads[:, D : 2 * D] = (
        over_frames(lambda i: spread(score_t[i, f]) * part(i, 0)) * SCALE
    ).astype(BF16)
    grads[:, 2 * D : 3 * D] = over_frames(
        lambda i: spread(shares_t[i, f]) * ga_t[frame_rows(i), :].astype(F32)
    ).astype(BF16)

    def put_out(at, value):
        cols = pl.ds(at, TILE)
        out_ref[:, cols] = (streams[mine, cols].astype(F32) + value).astype(BF16)

    backward(grads, pl.ds(0, 3 * D), 1, into(acc))
    rows_a[...] = (
        cot_ref[...].astype(F32) + rms_back(streams[mine, :].astype(F32), acc[...])
    ).astype(BF16)

    def put_ga(at, value):
        ga_win[own, pl.ds(at, TILE)] = value.astype(BF16)

    backward(rows_a, pl.ds(3 * D, D), 0, put_ga)
    deltas = per_head(ga_win[own, :].astype(F32) * att[...].astype(F32))
    dlt[...] = deltas.T[:16]
    leave(dlt_halo)
    for copies in ga_halo:
        leave(copies)

    def attend_back(hp):
        cols = cols_of(hp, 0)
        grad_two = stacked(ga_win[own, cols])
        weight = probs[hp]
        grad_prob = dot_nt(grad_two, qkv[:, cols_of(hp, 2)])
        row_delta = jnp.concatenate(column(deltas, hp), axis=0)
        score_grad = (weight * (grad_prob - row_delta)).astype(BF16)
        grads[:, cols] = (joined(dot(score_grad, qkv[:, cols_of(hp, 1)])) * SCALE).astype(BF16)
        middle = slice(ROWS, 2 * ROWS)
        gown[:, cols] = dot_tn(score_grad[:, middle], stacked(qkv[own, cols]))
        gown[:, cols_of(hp, 1)] = dot_tn(weight[:, middle].astype(BF16), grad_two)

    for hp in range(PAIRS):
        attend_back(hp)
    forward(attn_t, 1, 3 * D, D, put_out)
    backward(grads.at[:, pl.ds(0, D)], pl.ds(0, D), 0, into(acc))
    arrive(dlt_halo)

    def near_back(hp):
        cols = cols_of(hp, 0)
        grad_four = both_sides(ga_win, cols)
        weight = near_probs[hp]
        grad_prob = dot_nt(qkv[own, cols_of(hp, 2)], grad_four)
        score_grad = (weight * (grad_prob - near_lanes(dlt_got, hp))).astype(BF16)
        key_grad = gown[:, cols] + dot(score_grad, both_sides(qkv, cols))
        value_grad = gown[:, cols_of(hp, 1)] + dot(weight.astype(BF16), grad_four)
        grads[:, cols_of(hp, 1)] = (key_grad * SCALE).astype(BF16)
        grads[:, cols_of(hp, 2)] = value_grad.astype(BF16)

    for hp in range(PAIRS):
        if hp % 2 == 0:
            arrive(ga_halo[hp // 2])
        near_back(hp)

    def put_more(at, value):
        cols = pl.ds(at, TILE)
        acc[:, cols] = acc[:, cols] + value

    backward(grads.at[:, pl.ds(D, 2 * D)], pl.ds(D, 2 * D), 0, put_more)
    grad_ref[...] = (
        rows_a[...].astype(F32) + rms_back(x_ref[...].astype(F32), acc[...])
    ).astype(BF16)

    for copies in (x_halo, tot_halo, dlt_halo, *ga_halo):
        each_way(lambda way: copies[way].wait_send())
    for copy in cot_out + stream_out:
        copy.wait_send()
    if gathers:
        gather.close(0)
        gather.close(1)


def local(frames, count, frames_in, cotangent, w_qkv_space, w_out_space, w_qkv_time, w_out_time, neighbours):
    gathers = frames == 2 and count == 8 and w_qkv_space.shape[0] == 96
    blocks = [w_qkv_space, w_out_space, w_qkv_time, w_out_time]
    if not gathers:
        blocks = [lax.all_gather(block, "space", axis=0, tiled=True) for block in blocks]
    vmem = pl.BlockSpec(memory_space=pltpu.VMEM)
    hbm = pl.BlockSpec(memory_space=pl.ANY)
    dma = pltpu.SemaphoreType.DMA
    wide = (ROWS, 2 * D)
    out, grad = pl.pallas_call(
        functools.partial(kernel, frames, count, gathers),
        out_shape=[jax.ShapeDtypeStruct((ROWS, D), BF16)] * 2,
        in_specs=[vmem, vmem, hbm, hbm, hbm, hbm, pl.BlockSpec(memory_space=pltpu.SMEM)],
        out_specs=[vmem, vmem],
        scratch_shapes=[
            pltpu.VMEM((2, D, 4 * D), BF16),
            pltpu.VMEM((3 * ROWS, D), BF16),
            pltpu.VMEM((3 * ROWS, D), BF16),
            pltpu.VMEM((3 * ROWS, 3 * D), BF16),
            pltpu.VMEM((ROWS, D), BF16),
            pltpu.VMEM((PAIRS, 2 * ROWS, 3 * ROWS), F32),
            pltpu.VMEM((PAIRS, ROWS, 4 * ROWS), F32),
            *[pltpu.VMEM((frames * ROWS, D), BF16)] * 3,
            pltpu.VMEM((frames * ROWS, 3 * D), BF16),
            pltpu.VMEM((frames * ROWS, D), BF16),
            *[pltpu.VMEM((frames, frames, ROWS, 128), BF16)] * 2,
            pltpu.VMEM((ROWS, D), BF16),
            pltpu.VMEM((ROWS, D), BF16),
            pltpu.VMEM((ROWS, 3 * D), BF16),
            pltpu.VMEM(wide, F32),
            pltpu.VMEM((3 * ROWS, D), BF16),
            *[pltpu.VMEM((16, 128), F32), pltpu.VMEM((2, 16, 128), F32)] * 2,
            pltpu.VMEM((ROWS, D), F32),
            dma((4,)),
            dma((2, 2, 4)), dma((2, 4)), dma((2, 4)), dma((2, 4)),
            dma((2, 8)), dma((2, 8)), dma((2, 8)), dma((2, 8)),
            dma((2,)), dma((2,)), dma((2,)), dma((2,)),
            *[dma((3, 2))] * 2,
            *[dma((2,))] * 4,
            *[dma((frames - 1,)), dma((frames,))] * 2,
        ],
        compiler_params=pltpu.CompilerParams(
            collective_id=0, has_side_effects=True, vmem_limit_bytes=56 * 1024 * 1024
        ),
    )(frames_in[0], cotangent[0], *blocks, neighbours)
    return out[None], grad[None]


def solution(mesh):
    rows = P(("dp", "frame"), "space", None)
    held = P("space", None)
    return jax.shard_map(
        functools.partial(local, mesh.shape["frame"], mesh.shape["space"]),
        mesh=mesh,
        in_specs=(rows, rows, held, held, held, held, P()),
        out_specs=(rows, rows),
        check_vma=False,
    )
```

```python
import functools

import jax
import jax.numpy as jnp
from jax import lax
from jax.experimental import pallas as pl
from jax.experimental.pallas import tpu as pltpu
from jax.sharding import PartitionSpec as P

HEADS = 12
HD = 64
D = 768
ROWS = 128
PAIRS = HEADS // 2
EPS = 1e-06
FAR = -1e30
SCALE = HD ** (-0.5)
F32 = jnp.float32
BF16 = jnp.bfloat16
TILE = 256


def dot(a, b):
    return jnp.dot(a, b, preferred_element_type=F32)


def dot_nt(a, b):
    return lax.dot_general(a, b, (((1,), (1,)), ((), ())), preferred_element_type=F32)


def dot_tn(a, b):
    return lax.dot_general(a, b, (((0,), (0,)), ((), ())), preferred_element_type=F32)


def rms_factor(values):
    return lax.rsqrt(jnp.mean(values * values, axis=-1, keepdims=True) + EPS)


def rms_back(values, upstream):
    factor = rms_factor(values)
    inner = jnp.mean(values * upstream, axis=-1, keepdims=True)
    return factor * upstream - values * (factor * factor * factor * inner)


def remote(src, dst, send, recv, where):
    return pltpu.make_async_remote_copy(
        src_ref=src,
        dst_ref=dst,
        send_sem=send,
        recv_sem=recv,
        device_id=where,
        device_id_type=pl.DeviceIdType.MESH,
    )


class Gather:
    X = 2
    Z = 4

    def __init__(self, weights, sems):
        self.w = weights
        self.zs, self.zr, self.xs, self.xr, self.ys, self.yr, self.cs, self.cr, self.ps, self.pr = sems
        self.s = lax.axis_index("space")
        self.z = self.s // self.X
        self.x = self.s % self.X
        self.odd = lax.axis_index("frame")
        self.c = lax.axis_index("dp")

    def rows(self, group, shard, offset, count):
        start = pl.multiple_of(shard * 96 + offset, 16)
        return self.w.at[group, pl.ds(start, count), :]

    def main(self, group, shard):
        return self.rows(group, shard, 48 * self.c + 16 * self.odd, 32)

    def along_z(self, group, step, at):
        ref = self.main(group, at * self.X + self.x)
        way = 0 if step > 0 else 1
        return remote(
            ref, ref, self.zs.at[group, way, at], self.zr.at[group, at], {"space": self.s + step * self.X}
        )

    def along_x(self, group, at, column):
        ref = self.main(group, at * self.X + column)
        partner = self.s + 1 - 2 * self.x
        return remote(ref, ref, self.xs.at[group, at], self.xr.at[group, at], {"space": partner})

    def along_y(self, group, shard, sending):
        which = self.odd if sending else 1 - self.odd
        ref = self.rows(group, shard, 48 * self.c + 32 * which, 16)
        return remote(
            ref, ref, self.ys.at[group, shard], self.yr.at[group, shard], {"frame": 1 - self.odd}
        )

    def across(self, group, shard, sending):
        half = self.c if sending else 1 - self.c
        ref = self.rows(group, shard, 48 * half + 16 * self.odd, 32)
        return remote(
            ref, ref, self.cs.at[group, shard], self.cr.at[group, shard], {"dp": 1 - self.c}
        )

    def across_rest(self, group, shard, sending):
        half = self.c if sending else 1 - self.c
        ref = self.rows(group, shard, 48 * half + 32 * (1 - self.odd), 16)
        return remote(
            ref, ref, self.ps.at[group, shard], self.pr.at[group, shard], {"dp": 1 - self.c}
        )

    def open(self, group):
        @pl.when(self.z < self.Z - 1)
        def _():
            self.along_z(group, 1, self.z).start()

        @pl.when(self.z > 0)
        def _():
            self.along_z(group, -1, self.z).start()

        self.along_x(group, self.z, self.x).start()

    def z_step(self, group, distance):
        for step in (1, -1):
            at = self.z - step * distance

            @pl.when((at >= 0) & (at < self.Z))
            def _():
                self.along_z(group, -step, at).wait_recv()
                onward = (self.z + step >= 0) & (self.z + step < self.Z)

                @pl.when(onward)
                def _():
                    self.along_z(group, step, at).start()

                self.along_x(group, at, self.x).start()
                self.along_y(group, at * self.X + self.x, True).start()
                self.across(group, at * self.X + self.x, True).start()

    def x_step(self, group, distance):
        for step in (1, -1) if distance else (1,):
            at = self.z - step * distance

            @pl.when((at >= 0) & (at < self.Z))
            def _():
                self.along_x(group, at, 1 - self.x).wait_recv()
                self.along_y(group, at * self.X + 1 - self.x, True).start()
                self.across(group, at * self.X + 1 - self.x, True).start()

    def others(self):
        count = self.X * self.Z
        return [lax.rem(self.s + k, count) for k in range(1, count)]

    def y_stage(self, group):
        for shard in self.others():
            self.along_y(group, shard, False).wait_recv()
            self.across_rest(group, shard, True).start()

    def c_stage(self, group):
        for shard in self.others():
            self.across(group, shard, False).wait_recv()
            self.across_rest(group, shard, False).wait_recv()

    def close(self, group):
        for at in range(self.Z):

            @pl.when((self.z < self.Z - 1) & (at <= self.z))
            def _():
                self.along_z(group, 1, at).wait_send()

            @pl.when((self.z > 0) & (at >= self.z))
            def _():
                self.along_z(group, -1, at).wait_send()

            self.along_x(group, at, self.x).wait_send()
        for shard in self.others():
            self.along_y(group, shard, True).wait_send()
            self.across(group, shard, True).wait_send()
            self.across_rest(group, shard, True).wait_send()


def kernel(
    frames, count, gathers,
    x_ref, cot_ref, wqs_ref, wos_ref, wqt_ref, wot_ref, nb_ref,
    out_ref, grad_ref,
    weights, x_win, normed, qkv, att, probs, near_probs, streams, cots, normed_t, qkv_t, ga_t, shares_t, score_t,
    rows_a, attn_t, grads, gown, ga_win, tot, tot_got, dlt, dlt_got, acc,
    load_sem, zs, zr, xs, xr, ys, yr, cs, cr, ps, pr, hs, hr, bs, br, ds, dr, es, er, ts, tr, us, ur,
):
    s = lax.axis_index("space")
    f = lax.axis_index("frame")
    c = lax.axis_index("dp")

    barrier = pltpu.get_barrier_semaphore()
    peers = [{"space": lax.rem(s + k, count)} for k in (1, 2, count - 2, count - 1)]
    peers += [{"frame": lax.rem(f + k, frames)} for k in range(1, frames)]
    peers += [{"dp": 1 - c}]
    for peer in peers:
        pl.semaphore_signal(barrier, inc=1, device_id=peer, device_id_type=pl.DeviceIdType.MESH)

    depth = wqs_ref.shape[0]
    start = pl.multiple_of(s * depth, 16) if gathers else 0
    here = pl.ds(start, depth)
    loads = [
        pltpu.make_async_copy(ref, weights.at[group, here, pl.ds(col, ref.shape[1])], load_sem.at[i])
        for i, (ref, group, col) in enumerate(
            ((wqs_ref, 0, 0), (wos_ref, 0, 3 * D), (wqt_ref, 1, 0), (wot_ref, 1, 3 * D))
        )
    ]
    for load in loads:
        load.start()

    lane = lax.broadcasted_iota(jnp.int32, (1, 2 * HD), 1)
    first = lane < HD
    first_row = first.astype(F32).astype(BF16)
    second_row = (1.0 - first.astype(F32)).astype(BF16)

    def stacked(pair):
        return jnp.concatenate([pair * first_row, pair * second_row], axis=0)

    def joined(both):
        return jnp.where(first, both[:ROWS], both[ROWS:])

    def forward(rows, group, col, width, put):
        for at in range(0, width, TILE):
            put(at, dot(rows[...], weights[group, :, pl.ds(col + at, TILE)]))

    def backward(rows, cols, group, put):
        for at in range(0, D, TILE):
            put(at, dot_nt(rows[...], weights[group, pl.ds(at, TILE), cols]))

    def into(ref, col=0):
        def put(at, value):
            ref[:, pl.ds(col + at, TILE)] = value.astype(ref.dtype)

        return put

    own = pl.ds(ROWS, ROWS)
    sides = (pl.ds(0, ROWS), pl.ds(2 * ROWS, ROWS))
    has = [s > 0, s < count - 1]

    def two_ways(src, slots, send, recv):
        return [
            remote(src, slots[1 - way], send.at[way], recv.at[way], {"space": s + 2 * way - 1})
            for way in range(2)
        ]

    def each_way(action):
        for way in range(2):
            pl.when(has[way])(functools.partial(action, way))

    def leave(copies):
        each_way(lambda way: copies[way].start())

    def arrive(copies):
        each_way(lambda way: copies[1 - way].wait_recv())

    x_halo = two_ways(x_ref, [x_win.at[side, :] for side in sides], hs, hr)
    ga_halo = two_ways(ga_win.at[own, :], [ga_win.at[side, :] for side in sides], bs, br)
    tot_halo = two_ways(tot, [tot_got.at[way] for way in range(2)], ds, dr)
    dlt_halo = two_ways(dlt, [dlt_got.at[way] for way in range(2)], es, er)

    mine = pl.ds(pl.multiple_of(f * ROWS, ROWS), ROWS)

    def frame_copies(src, held, send, recv):
        out, got = [], []
        for k in range(1, frames):
            o = lax.rem(f + k, frames)
            theirs = pl.ds(pl.multiple_of(o * ROWS, ROWS), ROWS)
            where = {"frame": o}
            out.append(remote(src, held.at[mine, :], send.at[k - 1], recv.at[f], where))
            got.append(remote(src, held.at[theirs, :], send.at[k - 1], recv.at[o], where))
        return out, got

    cot_out, cot_got = frame_copies(cot_ref, cots, ts, tr)
    stream_out, stream_got = frame_copies(streams.at[mine, :], streams, us, ur)
    cots[mine, :] = cot_ref[...]
    x_win[own, :] = x_ref[...]
    for way in range(2):

        @pl.when(jnp.logical_not(has[way]))
        def _():
            x_win[sides[way], :] = jnp.zeros((ROWS, D), BF16)
            ga_win[sides[way], :] = jnp.zeros((ROWS, D), BF16)
            tot_got[way] = jnp.ones((16, 128), F32)
            dlt_got[way] = jnp.zeros((16, 128), F32)

    pl.semaphore_wait(barrier, len(peers))
    leave(x_halo)
    for copy in cot_out:
        copy.start()
    for load in loads:
        load.wait()
    gather = Gather(weights, (zs, zr, xs, xr, ys, yr, cs, cr, ps, pr)) if gathers else None

    def pass_on(*steps):
        if gathers:
            for name, *where in steps:
                getattr(gather, name)(*where)

    pass_on(
        ("open", 0),
        ("z_step", 0, 1), ("x_step", 0, 0), ("z_step", 0, 2), ("open", 1), ("x_step", 0, 1), ("z_step", 0, 3),
        ("x_step", 0, 2), ("z_step", 1, 1), ("x_step", 0, 3),
    )
    arrive(x_halo)
    values = x_win[...].astype(F32)
    normed[...] = (values * rms_factor(values)).astype(BF16)
    pass_on(("y_stage", 0), ("z_step", 1, 2), ("x_step", 1, 0), ("c_stage", 0))
    forward(normed, 0, 0, D, into(qkv))
    pass_on(("z_step", 1, 3), ("x_step", 1, 1))
    forward(normed, 0, D, 2 * D, into(qkv, D))
    pass_on(("x_step", 1, 2), ("x_step", 1, 3))

    def listed(block):
        hit = nb_ref[s, 0] == block
        for j in range(1, nb_ref.shape[1]):
            hit = hit | (nb_ref[s, j] == block)
        return jnp.where(hit, 0.0, FAR).astype(F32)

    key_lane = lax.broadcasted_iota(jnp.int32, (1, 3 * ROWS), 1)
    bias = jnp.where(
        key_lane < ROWS, listed(s - 1), jnp.where(key_lane < 2 * ROWS, listed(s), listed(s + 1))
    )

    head_lane = lax.broadcasted_iota(jnp.int32, (1, 128), 1)

    def cols_of(hp, part):
        return pl.ds(part * D + hp * 128, 128)

    def attend(hp, totals):
        cols = cols_of(hp, 0)
        scores = dot_nt(stacked(qkv[own, cols]), qkv[:, cols_of(hp, 1)]) * SCALE + bias
        expo = jnp.exp(scores)
        total = jnp.sum(expo, axis=-1, keepdims=True)
        weight = expo / total
        probs[hp] = weight
        att[:, cols] = joined(dot(weight.astype(BF16), qkv[:, cols_of(hp, 2)])).astype(BF16)
        totals = jnp.where(head_lane == 2 * hp, total[:ROWS], totals)
        return jnp.where(head_lane == 2 * hp + 1, total[ROWS:], totals)

    totals = jnp.ones((ROWS, 128), F32)
    for hp in range(PAIRS):
        totals = attend(hp, totals)
    tot[...] = totals.T[:16]
    leave(tot_halo)

    forward(att, 0, 3 * D, D, into(acc))
    streams[mine, :] = (x_ref[...].astype(F32) + acc[...]).astype(BF16)
    for copy in stream_out:
        copy.start()
    pass_on(("y_stage", 1))

    def listed_by(block):
        row = jnp.clip(block, 0, count - 1)
        hit = nb_ref[row, 0] == s
        for j in range(1, nb_ref.shape[1]):
            hit = hit | (nb_ref[row, j] == s)
        return jnp.where(hit & (block >= 0) & (block < count), 0.0, FAR).astype(F32)

    def both_sides(window, cols):
        return jnp.concatenate([stacked(window[side, cols]) for side in sides], axis=0)

    def column(held, hp):
        return [
            jnp.sum(jnp.where(head_lane == 2 * hp + i, held, 0.0), axis=-1, keepdims=True)
            for i in range(2)
        ]

    def near_lanes(held, hp):
        return jnp.concatenate(
            [held[way, 2 * hp + i : 2 * hp + i + 1, :] for way in range(2) for i in range(2)], axis=1
        )

    near_row = lax.broadcasted_iota(jnp.int32, (1, 4 * ROWS), 1)
    near_bias = jnp.where(near_row < 2 * ROWS, listed_by(s - 1), listed_by(s + 1))

    def near(hp):
        query_four = both_sides(qkv, cols_of(hp, 0))
        scores = dot_nt(qkv[own, cols_of(hp, 1)], query_four) * SCALE + near_bias
        near_probs[hp] = jnp.exp(scores) / near_lanes(tot_got, hp)

    arrive(tot_halo)
    for hp in range(PAIRS):
        near(hp)

    pass_on(("c_stage", 1))
    for copy in stream_got + cot_got:
        copy.wait_recv()
    values = streams[...].astype(F32)
    normed_t[...] = (values * rms_factor(values)).astype(BF16)
    forward(normed_t, 1, 0, 3 * D, into(qkv_t))
    backward(cots, pl.ds(3 * D, D), 1, into(ga_t))

    hot = (
        lax.broadcasted_iota(jnp.int32, (D, 128), 0) // HD
        == lax.broadcasted_iota(jnp.int32, (D, 128), 1)
    ).astype(F32).astype(BF16)

    def per_head(product):
        high = product.astype(BF16)
        low = (product - high.astype(F32)).astype(BF16)
        return dot(high, hot) + dot(low, hot)

    def spread(heads):
        return dot_nt(heads, hot)

    def frame_rows(i):
        return pl.ds(i * ROWS, ROWS)

    def part(i, which):
        return qkv_t[frame_rows(i), which * D : (which + 1) * D].astype(F32)

    for i in range(frames):
        query = part(i, 0)
        grad_att = ga_t[frame_rows(i), :].astype(F32)
        expos = [jnp.exp(per_head(query * part(g, 1)) * SCALE) for g in range(i + 1)]
        prob_grads = [per_head(grad_att * part(g, 2)) for g in range(i + 1)]
        total = sum(expos[1:], expos[0])
        shares = [expo / total for expo in expos]
        rounded = [share.astype(BF16) for share in shares]
        terms = [prob.astype(F32) * grad for prob, grad in zip(rounded, prob_grads)]
        delta = sum(terms[1:], terms[0])
        for g in range(frames):
            if g <= i:
                shares_t[i, g] = rounded[g]
                score_t[i, g] = (shares[g] * (prob_grads[g] - delta)).astype(BF16)
            else:
                shares_t[i, g] = jnp.zeros((ROWS, 128), BF16)
                score_t[i, g] = jnp.zeros((ROWS, 128), BF16)

    def over_frames(term):
        total = term(0)
        for i in range(1, frames):
            total = total + term(i)
        return total

    attn_t[...] = over_frames(lambda g: spread(shares_t[f, g]) * part(g, 2)).astype(BF16)
    grads[:, 0:D] = (over_frames(lambda g: spread(score_t[f, g]) * part(g, 1)) * SCALE).astype(BF16)
    grads[:, D : 2 * D] = (
        over_frames(lambda i: spread(score_t[i, f]) * part(i, 0)) * SCALE
    ).astype(BF16)
    grads[:, 2 * D : 3 * D] = over_frames(
        lambda i: spread(shares_t[i, f]) * ga_t[frame_rows(i), :].astype(F32)
    ).astype(BF16)

    def put_out(at, value):
        cols = pl.ds(at, TILE)
        out_ref[:, cols] = (streams[mine, cols].astype(F32) + value).astype(BF16)

    backward(grads, pl.ds(0, 3 * D), 1, into(acc))
    rows_a[...] = (
        cot_ref[...].astype(F32) + rms_back(streams[mine, :].astype(F32), acc[...])
    ).astype(BF16)

    def put_ga(at, value):
        ga_win[own, pl.ds(at, TILE)] = value.astype(BF16)

    backward(rows_a, pl.ds(3 * D, D), 0, put_ga)
    leave(ga_halo)
    deltas = per_head(ga_win[own, :].astype(F32) * att[...].astype(F32))
    dlt[...] = deltas.T[:16]
    leave(dlt_halo)

    def attend_back(hp):
        cols = cols_of(hp, 0)
        grad_two = stacked(ga_win[own, cols])
        weight = probs[hp]
        grad_prob = dot_nt(grad_two, qkv[:, cols_of(hp, 2)])
        row_delta = jnp.concatenate(column(deltas, hp), axis=0)
        score_grad = (weight * (grad_prob - row_delta)).astype(BF16)
        grads[:, cols] = (joined(dot(score_grad, qkv[:, cols_of(hp, 1)])) * SCALE).astype(BF16)
        middle = slice(ROWS, 2 * ROWS)
        gown[:, cols] = dot_tn(score_grad[:, middle], stacked(qkv[own, cols]))
        gown[:, cols_of(hp, 1)] = dot_tn(weight[:, middle].astype(BF16), grad_two)

    for hp in range(PAIRS):
        attend_back(hp)
    forward(attn_t, 1, 3 * D, D, put_out)
    backward(grads.at[:, pl.ds(0, D)], pl.ds(0, D), 0, into(acc))
    arrive(ga_halo)
    arrive(dlt_halo)

    def near_back(hp):
        cols = cols_of(hp, 0)
        grad_four = both_sides(ga_win, cols)
        weight = near_probs[hp]
        grad_prob = dot_nt(qkv[own, cols_of(hp, 2)], grad_four)
        score_grad = (weight * (grad_prob - near_lanes(dlt_got, hp))).astype(BF16)
        key_grad = gown[:, cols] + dot(score_grad, both_sides(qkv, cols))
        value_grad = gown[:, cols_of(hp, 1)] + dot(weight.astype(BF16), grad_four)
        grads[:, cols_of(hp, 1)] = (key_grad * SCALE).astype(BF16)
        grads[:, cols_of(hp, 2)] = value_grad.astype(BF16)

    for hp in range(PAIRS):
        near_back(hp)

    def put_more(at, value):
        cols = pl.ds(at, TILE)
        acc[:, cols] = acc[:, cols] + value

    backward(grads.at[:, pl.ds(D, 2 * D)], pl.ds(D, 2 * D), 0, put_more)
    grad_ref[...] = (
        rows_a[...].astype(F32) + rms_back(x_ref[...].astype(F32), acc[...])
    ).astype(BF16)

    for copies in (x_halo, tot_halo, ga_halo, dlt_halo):
        each_way(lambda way: copies[way].wait_send())
    for copy in cot_out + stream_out:
        copy.wait_send()
    if gathers:
        gather.close(0)
        gather.close(1)


def local(frames, count, frames_in, cotangent, w_qkv_space, w_out_space, w_qkv_time, w_out_time, neighbours):
    gathers = frames == 2 and count == 8 and w_qkv_space.shape[0] == 96
    blocks = [w_qkv_space, w_out_space, w_qkv_time, w_out_time]
    if not gathers:
        blocks = [lax.all_gather(block, "space", axis=0, tiled=True) for block in blocks]
    vmem = pl.BlockSpec(memory_space=pltpu.VMEM)
    hbm = pl.BlockSpec(memory_space=pl.ANY)
    dma = pltpu.SemaphoreType.DMA
    wide = (ROWS, 2 * D)
    out, grad = pl.pallas_call(
        functools.partial(kernel, frames, count, gathers),
        out_shape=[jax.ShapeDtypeStruct((ROWS, D), BF16)] * 2,
        in_specs=[vmem, vmem, hbm, hbm, hbm, hbm, pl.BlockSpec(memory_space=pltpu.SMEM)],
        out_specs=[vmem, vmem],
        scratch_shapes=[
            pltpu.VMEM((2, D, 4 * D), BF16),
            pltpu.VMEM((3 * ROWS, D), BF16),
            pltpu.VMEM((3 * ROWS, D), BF16),
            pltpu.VMEM((3 * ROWS, 3 * D), BF16),
            pltpu.VMEM((ROWS, D), BF16),
            pltpu.VMEM((PAIRS, 2 * ROWS, 3 * ROWS), F32),
            pltpu.VMEM((PAIRS, ROWS, 4 * ROWS), F32),
            *[pltpu.VMEM((frames * ROWS, D), BF16)] * 3,
            pltpu.VMEM((frames * ROWS, 3 * D), BF16),
            pltpu.VMEM((frames * ROWS, D), BF16),
            *[pltpu.VMEM((frames, frames, ROWS, 128), BF16)] * 2,
            pltpu.VMEM((ROWS, D), BF16),
            pltpu.VMEM((ROWS, D), BF16),
            pltpu.VMEM((ROWS, 3 * D), BF16),
            pltpu.VMEM(wide, F32),
            pltpu.VMEM((3 * ROWS, D), BF16),
            *[pltpu.VMEM((16, 128), F32), pltpu.VMEM((2, 16, 128), F32)] * 2,
            pltpu.VMEM((ROWS, D), F32),
            dma((4,)),
            dma((2, 2, 4)), dma((2, 4)), dma((2, 4)), dma((2, 4)),
            dma((2, 8)), dma((2, 8)), dma((2, 8)), dma((2, 8)),
            dma((2, 8)), dma((2, 8)),
            *[dma((2,))] * 8,
            *[dma((frames - 1,)), dma((frames,))] * 2,
        ],
        compiler_params=pltpu.CompilerParams(
            collective_id=0, has_side_effects=True, vmem_limit_bytes=56 * 1024 * 1024
        ),
    )(frames_in[0], cotangent[0], *blocks, neighbours)
    return out[None], grad[None]


def solution(mesh):
    rows = P(("dp", "frame"), "space", None)
    held = P("space", None)
    return jax.shard_map(
        functools.partial(local, mesh.shape["frame"], mesh.shape["space"]),
        mesh=mesh,
        in_specs=(rows, rows, held, held, held, held, P()),
        out_specs=(rows, rows),
        check_vma=False,
    )
```

```python
import functools

import jax
import jax.numpy as jnp
from jax import lax
from jax.experimental import pallas as pl
from jax.experimental.pallas import tpu as pltpu
from jax.sharding import PartitionSpec as P

HEADS = 12
HD = 64
D = 768
ROWS = 128
PAIRS = HEADS // 2
EPS = 1e-06
FAR = -1e30
SCALE = HD ** (-0.5)
F32 = jnp.float32
BF16 = jnp.bfloat16
TILE = 256


def dot(a, b):
    return jnp.dot(a, b, preferred_element_type=F32)


def dot_nt(a, b):
    return lax.dot_general(a, b, (((1,), (1,)), ((), ())), preferred_element_type=F32)


def dot_tn(a, b):
    return lax.dot_general(a, b, (((0,), (0,)), ((), ())), preferred_element_type=F32)


def rms_factor(values):
    return lax.rsqrt(jnp.mean(values * values, axis=-1, keepdims=True) + EPS)


def rms_back(values, upstream):
    factor = rms_factor(values)
    inner = jnp.mean(values * upstream, axis=-1, keepdims=True)
    return factor * upstream - values * (factor * factor * factor * inner)


def remote(src, dst, send, recv, where):
    return pltpu.make_async_remote_copy(
        src_ref=src,
        dst_ref=dst,
        send_sem=send,
        recv_sem=recv,
        device_id=where,
        device_id_type=pl.DeviceIdType.MESH,
    )


class Gather:
    X = 2
    Z = 4

    def __init__(self, weights, sems):
        self.w = weights
        self.zs, self.zr, self.xs, self.xr, self.ys, self.yr, self.cs, self.cr = sems
        self.s = lax.axis_index("space")
        self.z = self.s // self.X
        self.x = self.s % self.X
        self.odd = lax.axis_index("frame")
        self.c = lax.axis_index("dp")

    def rows(self, group, shard, offset, count):
        start = pl.multiple_of(shard * 96 + offset, 16)
        return self.w.at[group, pl.ds(start, count), :]

    def main(self, group, shard):
        return self.rows(group, shard, 48 * self.c + 16 * self.odd, 32)

    def along_z(self, group, step, at):
        ref = self.main(group, at * self.X + self.x)
        way = 0 if step > 0 else 1
        return remote(
            ref, ref, self.zs.at[group, way, at], self.zr.at[group, at], {"space": self.s + step * self.X}
        )

    def along_x(self, group, at, column):
        ref = self.main(group, at * self.X + column)
        partner = self.s + 1 - 2 * self.x
        return remote(ref, ref, self.xs.at[group, at], self.xr.at[group, at], {"space": partner})

    def along_y(self, group, shard, sending):
        which = self.odd if sending else 1 - self.odd
        ref = self.rows(group, shard, 48 * self.c + 32 * which, 16)
        return remote(
            ref, ref, self.ys.at[group, shard], self.yr.at[group, shard], {"frame": 1 - self.odd}
        )

    def across(self, group, shard, sending):
        half = self.c if sending else 1 - self.c
        ref = self.rows(group, shard, 48 * half, 48)
        return remote(
            ref, ref, self.cs.at[group, shard], self.cr.at[group, shard], {"dp": 1 - self.c}
        )

    def open(self, group):
        @pl.when(self.z < self.Z - 1)
        def _():
            self.along_z(group, 1, self.z).start()

        @pl.when(self.z > 0)
        def _():
            self.along_z(group, -1, self.z).start()

        self.along_x(group, self.z, self.x).start()

    def z_step(self, group, distance):
        for step in (1, -1):
            at = self.z - step * distance

            @pl.when((at >= 0) & (at < self.Z))
            def _():
                self.along_z(group, -step, at).wait_recv()
                onward = (self.z + step >= 0) & (self.z + step < self.Z)

                @pl.when(onward)
                def _():
                    self.along_z(group, step, at).start()

                self.along_x(group, at, self.x).start()
                self.along_y(group, at * self.X + self.x, True).start()

    def x_step(self, group, distance):
        for step in (1, -1) if distance else (1,):
            at = self.z - step * distance

            @pl.when((at >= 0) & (at < self.Z))
            def _():
                self.along_x(group, at, 1 - self.x).wait_recv()
                self.along_y(group, at * self.X + 1 - self.x, True).start()

    def others(self):
        count = self.X * self.Z
        return [lax.rem(self.s + k, count) for k in range(1, count)]

    def y_stage(self, group):
        for shard in self.others():
            self.along_y(group, shard, False).wait_recv()
            self.across(group, shard, True).start()

    def c_stage(self, group):
        for shard in self.others():
            self.across(group, shard, False).wait_recv()

    def close(self, group):
        for at in range(self.Z):

            @pl.when((self.z < self.Z - 1) & (at <= self.z))
            def _():
                self.along_z(group, 1, at).wait_send()

            @pl.when((self.z > 0) & (at >= self.z))
            def _():
                self.along_z(group, -1, at).wait_send()

            self.along_x(group, at, self.x).wait_send()
        for shard in self.others():
            self.along_y(group, shard, True).wait_send()
            self.across(group, shard, True).wait_send()


def kernel(
    frames, count, gathers,
    x_ref, cot_ref, wqs_ref, wos_ref, wqt_ref, wot_ref, nb_ref,
    out_ref, grad_ref,
    weights, x_win, normed, qkv, att, probs, near_probs, streams, cots, normed_t, qkv_t, ga_t, shares_t, score_t,
    rows_a, attn_t, grads, gown, ga_win, tot, tot_got, dlt, dlt_got, acc,
    load_sem, zs, zr, xs, xr, ys, yr, cs, cr, hs, hr, bs, br, ds, dr, es, er, ts, tr, us, ur,
):
    s = lax.axis_index("space")
    f = lax.axis_index("frame")
    c = lax.axis_index("dp")

    barrier = pltpu.get_barrier_semaphore()
    peers = [{"space": lax.rem(s + k, count)} for k in (1, 2, count - 2, count - 1)]
    peers += [{"frame": lax.rem(f + k, frames)} for k in range(1, frames)]
    peers += [{"dp": 1 - c}]
    for peer in peers:
        pl.semaphore_signal(barrier, inc=1, device_id=peer, device_id_type=pl.DeviceIdType.MESH)

    depth = wqs_ref.shape[0]
    start = pl.multiple_of(s * depth, 16) if gathers else 0
    here = pl.ds(start, depth)
    loads = [
        pltpu.make_async_copy(ref, weights.at[group, here, pl.ds(col, ref.shape[1])], load_sem.at[i])
        for i, (ref, group, col) in enumerate(
            ((wqs_ref, 0, 0), (wos_ref, 0, 3 * D), (wqt_ref, 1, 0), (wot_ref, 1, 3 * D))
        )
    ]
    for load in loads:
        load.start()

    lane = lax.broadcasted_iota(jnp.int32, (1, 2 * HD), 1)
    first = lane < HD
    first_row = first.astype(F32).astype(BF16)
    second_row = (1.0 - first.astype(F32)).astype(BF16)

    def stacked(pair):
        return jnp.concatenate([pair * first_row, pair * second_row], axis=0)

    def joined(both):
        return jnp.where(first, both[:ROWS], both[ROWS:])

    def forward(rows, group, col, width, put):
        for at in range(0, width, TILE):
            put(at, dot(rows[...], weights[group, :, pl.ds(col + at, TILE)]))

    def backward(rows, cols, group, put):
        for at in range(0, D, TILE):
            put(at, dot_nt(rows[...], weights[group, pl.ds(at, TILE), cols]))

    def into(ref, col=0):
        def put(at, value):
            ref[:, pl.ds(col + at, TILE)] = value.astype(ref.dtype)

        return put

    own = pl.ds(ROWS, ROWS)
    sides = (pl.ds(0, ROWS), pl.ds(2 * ROWS, ROWS))
    has = [s > 0, s < count - 1]

    def two_ways(src, slots, send, recv):
        return [
            remote(src, slots[1 - way], send.at[way], recv.at[way], {"space": s + 2 * way - 1})
            for way in range(2)
        ]

    def each_way(action):
        for way in range(2):
            pl.when(has[way])(functools.partial(action, way))

    def leave(copies):
        each_way(lambda way: copies[way].start())

    def arrive(copies):
        each_way(lambda way: copies[1 - way].wait_recv())

    x_halo = two_ways(x_ref, [x_win.at[side, :] for side in sides], hs, hr)
    ga_halo = two_ways(ga_win.at[own, :], [ga_win.at[side, :] for side in sides], bs, br)
    tot_halo = two_ways(tot, [tot_got.at[way] for way in range(2)], ds, dr)
    dlt_halo = two_ways(dlt, [dlt_got.at[way] for way in range(2)], es, er)

    mine = pl.ds(pl.multiple_of(f * ROWS, ROWS), ROWS)

    def frame_copies(src, held, send, recv):
        out, got = [], []
        for k in range(1, frames):
            o = lax.rem(f + k, frames)
            theirs = pl.ds(pl.multiple_of(o * ROWS, ROWS), ROWS)
            where = {"frame": o}
            out.append(remote(src, held.at[mine, :], send.at[k - 1], recv.at[f], where))
            got.append(remote(src, held.at[theirs, :], send.at[k - 1], recv.at[o], where))
        return out, got

    cot_out, cot_got = frame_copies(cot_ref, cots, ts, tr)
    stream_out, stream_got = frame_copies(streams.at[mine, :], streams, us, ur)
    cots[mine, :] = cot_ref[...]
    x_win[own, :] = x_ref[...]
    for way in range(2):

        @pl.when(jnp.logical_not(has[way]))
        def _():
            x_win[sides[way], :] = jnp.zeros((ROWS, D), BF16)
            ga_win[sides[way], :] = jnp.zeros((ROWS, D), BF16)
            tot_got[way] = jnp.ones((16, 128), F32)
            dlt_got[way] = jnp.zeros((16, 128), F32)

    pl.semaphore_wait(barrier, len(peers))
    leave(x_halo)
    for copy in cot_out:
        copy.start()
    for load in loads:
        load.wait()
    gather = Gather(weights, (zs, zr, xs, xr, ys, yr, cs, cr)) if gathers else None

    def pass_on(*steps):
        if gathers:
            for name, *where in steps:
                getattr(gather, name)(*where)

    pass_on(
        ("open", 0),
        ("z_step", 0, 1), ("x_step", 0, 0), ("z_step", 0, 2), ("open", 1), ("x_step", 0, 1), ("z_step", 0, 3),
        ("x_step", 0, 2), ("z_step", 1, 1), ("x_step", 0, 3),
    )
    arrive(x_halo)
    values = x_win[...].astype(F32)
    normed[...] = (values * rms_factor(values)).astype(BF16)
    pass_on(("y_stage", 0), ("z_step", 1, 2), ("x_step", 1, 0), ("c_stage", 0))
    forward(normed, 0, 0, D, into(qkv))
    pass_on(("z_step", 1, 3), ("x_step", 1, 1))
    forward(normed, 0, D, 2 * D, into(qkv, D))
    pass_on(("x_step", 1, 2))

    def listed(block):
        hit = nb_ref[s, 0] == block
        for j in range(1, nb_ref.shape[1]):
            hit = hit | (nb_ref[s, j] == block)
        return jnp.where(hit, 0.0, FAR).astype(F32)

    key_lane = lax.broadcasted_iota(jnp.int32, (1, 3 * ROWS), 1)
    bias = jnp.where(
        key_lane < ROWS, listed(s - 1), jnp.where(key_lane < 2 * ROWS, listed(s), listed(s + 1))
    )

    head_lane = lax.broadcasted_iota(jnp.int32, (1, 128), 1)

    def cols_of(hp, part):
        return pl.ds(part * D + hp * 128, 128)

    def attend(hp, totals):
        cols = cols_of(hp, 0)
        scores = dot_nt(stacked(qkv[own, cols]), qkv[:, cols_of(hp, 1)]) * SCALE + bias
        expo = jnp.exp(scores)
        total = jnp.sum(expo, axis=-1, keepdims=True)
        weight = expo / total
        probs[hp] = weight
        att[:, cols] = joined(dot(weight.astype(BF16), qkv[:, cols_of(hp, 2)])).astype(BF16)
        totals = jnp.where(head_lane == 2 * hp, total[:ROWS], totals)
        return jnp.where(head_lane == 2 * hp + 1, total[ROWS:], totals)

    totals = jnp.ones((ROWS, 128), F32)
    for hp in range(PAIRS):
        totals = attend(hp, totals)
    tot[...] = totals.T[:16]
    leave(tot_halo)
    pass_on(("x_step", 1, 3))

    forward(att, 0, 3 * D, D, into(acc))
    streams[mine, :] = (x_ref[...].astype(F32) + acc[...]).astype(BF16)
    for copy in stream_out:
        copy.start()
    pass_on(("y_stage", 1))

    def listed_by(block):
        row = jnp.clip(block, 0, count - 1)
        hit = nb_ref[row, 0] == s
        for j in range(1, nb_ref.shape[1]):
            hit = hit | (nb_ref[row, j] == s)
        return jnp.where(hit & (block >= 0) & (block < count), 0.0, FAR).astype(F32)

    def both_sides(window, cols):
        return jnp.concatenate([stacked(window[side, cols]) for side in sides], axis=0)

    def column(held, hp):
        return [
            jnp.sum(jnp.where(head_lane == 2 * hp + i, held, 0.0), axis=-1, keepdims=True)
            for i in range(2)
        ]

    def near_lanes(held, hp):
        return jnp.concatenate(
            [held[way, 2 * hp + i : 2 * hp + i + 1, :] for way in range(2) for i in range(2)], axis=1
        )

    near_row = lax.broadcasted_iota(jnp.int32, (1, 4 * ROWS), 1)
    near_bias = jnp.where(near_row < 2 * ROWS, listed_by(s - 1), listed_by(s + 1))

    def near(hp):
        query_four = both_sides(qkv, cols_of(hp, 0))
        scores = dot_nt(qkv[own, cols_of(hp, 1)], query_four) * SCALE + near_bias
        near_probs[hp] = jnp.exp(scores) / near_lanes(tot_got, hp)

    arrive(tot_halo)
    for hp in range(PAIRS):
        near(hp)

    pass_on(("c_stage", 1))
    for copy in stream_got + cot_got:
        copy.wait_recv()
    values = streams[...].astype(F32)
    normed_t[...] = (values * rms_factor(values)).astype(BF16)
    forward(normed_t, 1, 0, 3 * D, into(qkv_t))
    backward(cots, pl.ds(3 * D, D), 1, into(ga_t))

    hot = (
        lax.broadcasted_iota(jnp.int32, (D, 128), 0) // HD
        == lax.broadcasted_iota(jnp.int32, (D, 128), 1)
    ).astype(F32).astype(BF16)

    def per_head(product):
        high = product.astype(BF16)
        low = (product - high.astype(F32)).astype(BF16)
        return dot(high, hot) + dot(low, hot)

    def spread(heads):
        return dot_nt(heads, hot)

    def frame_rows(i):
        return pl.ds(i * ROWS, ROWS)

    def part(i, which):
        return qkv_t[frame_rows(i), which * D : (which + 1) * D].astype(F32)

    for i in range(frames):
        query = part(i, 0)
        grad_att = ga_t[frame_rows(i), :].astype(F32)
        expos = [jnp.exp(per_head(query * part(g, 1)) * SCALE) for g in range(i + 1)]
        prob_grads = [per_head(grad_att * part(g, 2)) for g in range(i + 1)]
        total = sum(expos[1:], expos[0])
        shares = [expo / total for expo in expos]
        rounded = [share.astype(BF16) for share in shares]
        terms = [prob.astype(F32) * grad for prob, grad in zip(rounded, prob_grads)]
        delta = sum(terms[1:], terms[0])
        for g in range(frames):
            if g <= i:
                shares_t[i, g] = rounded[g]
                score_t[i, g] = (shares[g] * (prob_grads[g] - delta)).astype(BF16)
            else:
                shares_t[i, g] = jnp.zeros((ROWS, 128), BF16)
                score_t[i, g] = jnp.zeros((ROWS, 128), BF16)

    def over_frames(term):
        total = term(0)
        for i in range(1, frames):
            total = total + term(i)
        return total

    attn_t[...] = over_frames(lambda g: spread(shares_t[f, g]) * part(g, 2)).astype(BF16)
    grads[:, 0:D] = (over_frames(lambda g: spread(score_t[f, g]) * part(g, 1)) * SCALE).astype(BF16)
    grads[:, D : 2 * D] = (
        over_frames(lambda i: spread(score_t[i, f]) * part(i, 0)) * SCALE
    ).astype(BF16)
    grads[:, 2 * D : 3 * D] = over_frames(
        lambda i: spread(shares_t[i, f]) * ga_t[frame_rows(i), :].astype(F32)
    ).astype(BF16)

    def put_out(at, value):
        cols = pl.ds(at, TILE)
        out_ref[:, cols] = (streams[mine, cols].astype(F32) + value).astype(BF16)

    backward(grads, pl.ds(0, 3 * D), 1, into(acc))
    rows_a[...] = (
        cot_ref[...].astype(F32) + rms_back(streams[mine, :].astype(F32), acc[...])
    ).astype(BF16)

    def put_ga(at, value):
        ga_win[own, pl.ds(at, TILE)] = value.astype(BF16)

    backward(rows_a, pl.ds(3 * D, D), 0, put_ga)
    leave(ga_halo)
    deltas = per_head(ga_win[own, :].astype(F32) * att[...].astype(F32))
    dlt[...] = deltas.T[:16]
    leave(dlt_halo)

    def attend_back(hp):
        cols = cols_of(hp, 0)
        grad_two = stacked(ga_win[own, cols])
        weight = probs[hp]
        grad_prob = dot_nt(grad_two, qkv[:, cols_of(hp, 2)])
        row_delta = jnp.concatenate(column(deltas, hp), axis=0)
        score_grad = (weight * (grad_prob - row_delta)).astype(BF16)
        grads[:, cols] = (joined(dot(score_grad, qkv[:, cols_of(hp, 1)])) * SCALE).astype(BF16)
        middle = slice(ROWS, 2 * ROWS)
        gown[:, cols] = dot_tn(score_grad[:, middle], stacked(qkv[own, cols]))
        gown[:, cols_of(hp, 1)] = dot_tn(weight[:, middle].astype(BF16), grad_two)

    for hp in range(PAIRS):
        attend_back(hp)
    forward(attn_t, 1, 3 * D, D, put_out)
    backward(grads.at[:, pl.ds(0, D)], pl.ds(0, D), 0, into(acc))
    arrive(ga_halo)
    arrive(dlt_halo)

    def near_back(hp):
        cols = cols_of(hp, 0)
        grad_four = both_sides(ga_win, cols)
        weight = near_probs[hp]
        grad_prob = dot_nt(qkv[own, cols_of(hp, 2)], grad_four)
        score_grad = (weight * (grad_prob - near_lanes(dlt_got, hp))).astype(BF16)
        key_grad = gown[:, cols] + dot(score_grad, both_sides(qkv, cols))
        value_grad = gown[:, cols_of(hp, 1)] + dot(weight.astype(BF16), grad_four)
        grads[:, cols_of(hp, 1)] = (key_grad * SCALE).astype(BF16)
        grads[:, cols_of(hp, 2)] = value_grad.astype(BF16)

    for hp in range(PAIRS):
        near_back(hp)

    def put_more(at, value):
        cols = pl.ds(at, TILE)
        acc[:, cols] = acc[:, cols] + value

    backward(grads.at[:, pl.ds(D, 2 * D)], pl.ds(D, 2 * D), 0, put_more)
    grad_ref[...] = (
        rows_a[...].astype(F32) + rms_back(x_ref[...].astype(F32), acc[...])
    ).astype(BF16)

    for copies in (x_halo, tot_halo, ga_halo, dlt_halo):
        each_way(lambda way: copies[way].wait_send())
    for copy in cot_out + stream_out:
        copy.wait_send()
    if gathers:
        gather.close(0)
        gather.close(1)


def local(frames, count, frames_in, cotangent, w_qkv_space, w_out_space, w_qkv_time, w_out_time, neighbours):
    gathers = frames == 2 and count == 8 and w_qkv_space.shape[0] == 96
    blocks = [w_qkv_space, w_out_space, w_qkv_time, w_out_time]
    if not gathers:
        blocks = [lax.all_gather(block, "space", axis=0, tiled=True) for block in blocks]
    vmem = pl.BlockSpec(memory_space=pltpu.VMEM)
    hbm = pl.BlockSpec(memory_space=pl.ANY)
    dma = pltpu.SemaphoreType.DMA
    wide = (ROWS, 2 * D)
    out, grad = pl.pallas_call(
        functools.partial(kernel, frames, count, gathers),
        out_shape=[jax.ShapeDtypeStruct((ROWS, D), BF16)] * 2,
        in_specs=[vmem, vmem, hbm, hbm, hbm, hbm, pl.BlockSpec(memory_space=pltpu.SMEM)],
        out_specs=[vmem, vmem],
        scratch_shapes=[
            pltpu.VMEM((2, D, 4 * D), BF16),
            pltpu.VMEM((3 * ROWS, D), BF16),
            pltpu.VMEM((3 * ROWS, D), BF16),
            pltpu.VMEM((3 * ROWS, 3 * D), BF16),
            pltpu.VMEM((ROWS, D), BF16),
            pltpu.VMEM((PAIRS, 2 * ROWS, 3 * ROWS), F32),
            pltpu.VMEM((PAIRS, ROWS, 4 * ROWS), F32),
            *[pltpu.VMEM((frames * ROWS, D), BF16)] * 3,
            pltpu.VMEM((frames * ROWS, 3 * D), BF16),
            pltpu.VMEM((frames * ROWS, D), BF16),
            *[pltpu.VMEM((frames, frames, ROWS, 128), BF16)] * 2,
            pltpu.VMEM((ROWS, D), BF16),
            pltpu.VMEM((ROWS, D), BF16),
            pltpu.VMEM((ROWS, 3 * D), BF16),
            pltpu.VMEM(wide, F32),
            pltpu.VMEM((3 * ROWS, D), BF16),
            *[pltpu.VMEM((16, 128), F32), pltpu.VMEM((2, 16, 128), F32)] * 2,
            pltpu.VMEM((ROWS, D), F32),
            dma((4,)),
            dma((2, 2, 4)), dma((2, 4)), dma((2, 4)), dma((2, 4)),
            dma((2, 8)), dma((2, 8)), dma((2, 8)), dma((2, 8)),
            *[dma((2,))] * 8,
            *[dma((frames - 1,)), dma((frames,))] * 2,
        ],
        compiler_params=pltpu.CompilerParams(
            collective_id=0, has_side_effects=True, vmem_limit_bytes=56 * 1024 * 1024
        ),
    )(frames_in[0], cotangent[0], *blocks, neighbours)
    return out[None], grad[None]


def solution(mesh):
    rows = P(("dp", "frame"), "space", None)
    held = P("space", None)
    return jax.shard_map(
        functools.partial(local, mesh.shape["frame"], mesh.shape["space"]),
        mesh=mesh,
        in_specs=(rows, rows, held, held, held, held, P()),
        out_specs=(rows, rows),
        check_vma=False,
    )
```
